512 devices in a mesh: tm: 64 (over z, x, core), runs: 8 (over y).
Axes of the slice: x: 4, y: 8, z: 8, core: 2. Of those that a mesh axis runs over, the one named last changes fastest.
Arguments:
- samples: float32 [16, 131072, 128], P('runs', 'tm'), may hold values from -24 to 24, as said below
- cohesion: int32 [16], replicated, may hold values from 0 to 3
- rolling: int32 [16], replicated, may hold values from 0 to 3
Outputs:
- level_mean: float32 [4, 64, 2, 128, 128], P(None, 'tm')
- level_spread: float32 [4, 64, 128, 128], P(None, 'tm')
- roll_mean: float32 [4, 64, 2, 128, 128], P(None, 'tm')
The draws below stay inside these ranges and needn't reach their ends.
Inputs may be any that keep to these rules, and one draw needn't show every extreme that they name: `samples`: each channel of each run is filtered noise with a gain of its own and correlation with the next channel.
All inputs are finite; a program needn't handle non-finite values.
Results may differ from the reference program's by a relative error of at most 0.00016.
Values sent between devices are 32-bit elements; how exact they have to be, the bound alone decides.
No kernel may reach another device: no remote copies, remote signals or barrier semaphores. Data moves between devices by JAX's collectives and lax.ppermute only.
A program may use at most 64 MiB of HBM per device.

```python
import math
import jax
import jax.numpy as jnp
from jax import lax

CH = 128
BIN = 1024
NC = 4
NQ = 4
SAMPLES = 131072
RUNS = 16
NB = 64


def draw_samples(key, part):
    key = jax.random.fold_in(key, 11)
    keys = jax.random.split(key, 3)
    noise = jax.random.truncated_normal(keys[0], -4.0, 4.0, (RUNS, SAMPLES + 1, CH + 1), jnp.float32)
    gains = jnp.exp(jax.random.uniform(keys[1], (RUNS, 1, CH), jnp.float32, math.log(0.5), math.log(2.0)))
    taps = jax.random.uniform(keys[2], (RUNS, 1, CH), jnp.float32, -0.8, 0.8)
    mixed = noise[:, :, :CH] + 0.6 * noise[:, :, 1:]
    shaped = mixed[:, 1:] + taps * mixed[:, :-1]
    return gains * shaped


def touch_ends(drawn, rng, smallest, high):
    longest = drawn.shape.index(max(drawn.shape))
    spots = []
    for shift in (0, 1):
        where = [jax.random.randint(jax.random.fold_in(rng, axis), (), 0, length) for axis, length in enumerate(drawn.shape)]
        where[longest] = (where[longest] + shift) % drawn.shape[longest]
        spots.append(tuple(where))
    return drawn.at[spots[0]].set(smallest).at[spots[1]].set(high)


def setup_inputs(seed: int = 0) -> dict:
    splits = jax.random.split(jax.random.key(seed), 4)
    samples = draw_samples(jax.random.fold_in(splits[3], 71), 0)
    cohesion = touch_ends(jax.random.randint(splits[1], (RUNS,), 0, NC), jax.random.fold_in(splits[1], 1), 0, NC - 1).astype(jnp.int32)
    rolling = touch_ends(jax.random.randint(splits[2], (RUNS,), 0, NQ), jax.random.fold_in(splits[2], 1), 0, NQ - 1).astype(jnp.int32)
    return dict(samples=samples, cohesion=cohesion, rolling=rolling)


def level_onehot(levels, level_count):
    return (levels[:, None] == jnp.arange(level_count, dtype=jnp.int32)[None, :]).astype(jnp.float32)


def reference(samples, cohesion, rolling):
    t_pos = jnp.arange(SAMPLES, dtype=jnp.float32)
    window = 0.5 - 0.5 * jnp.cos(2.0 * math.pi * t_pos / SAMPLES)
    norm_scale = 1.0 / (0.375 * BIN * SAMPLES)

    def one_run(signal):
        spectrum = jnp.fft.fft(signal * window[:, None], axis=0)[: SAMPLES // 2]
        stacked_parts = jnp.concatenate([jnp.real(spectrum), jnp.imag(spectrum)], axis=1)
        stacked_parts = stacked_parts.reshape(NB, BIN, 2 * CH)
        product_matrix = jnp.einsum("owa,owh->oah", stacked_parts, stacked_parts, precision=lax.Precision.HIGHEST)
        cross_re = product_matrix[:, :CH, :CH] + product_matrix[:, CH:, CH:]
        cross_im = product_matrix[:, CH:, :CH] - product_matrix[:, :CH, CH:]
        return jnp.stack([cross_re, cross_im], axis=1) * norm_scale

    cross = lax.map(one_run, samples)
    onehot = level_onehot(cohesion, NC)
    counts = jnp.sum(onehot, axis=0)
    level_sum = jnp.einsum("rl,rbxij->lbxij", onehot, cross, precision=lax.Precision.HIGHEST)
    level_mean = level_sum / jnp.maximum(counts, 1.0)[:, None, None, None, None]
    spread_offset = cross[:, None] - level_mean[None]
    squares = jnp.sum(spread_offset * spread_offset, axis=3)
    level_spread = BIN * jnp.einsum("rl,rlbij->lbij", onehot, squares, precision=lax.Precision.HIGHEST)
    roll_hot = level_onehot(rolling, NQ)
    roll_counts = jnp.sum(roll_hot, axis=0)
    roll_sum = jnp.einsum("rl,rbxij->lbxij", roll_hot, cross, precision=lax.Precision.HIGHEST)
    roll_mean = roll_sum / jnp.maximum(roll_counts, 1.0)[:, None, None, None, None]
    return level_mean, level_spread, roll_mean
```

```python
import functools
import math

import jax
import jax.numpy as jnp
import ml_dtypes
import numpy as np
from jax import lax
from jax.experimental import pallas as pl
from jax.experimental.pallas import tpu as pltpu
from jax.sharding import PartitionSpec as P

CH = 128
BIN = 1024
NC = 4
NQ = 4
TOTAL = 131072
RUNS = 16
NB = 64
T1 = 512
T2 = 256

NT = (((1,), (1,)), ((), ()))
MIB = 1 << 20


def split_table(table):
    high = table.astype(ml_dtypes.bfloat16)
    low = (table - high.astype(np.float64)).astype(ml_dtypes.bfloat16)
    return high, low


@functools.lru_cache(maxsize=None)
def tables():
    k1 = np.arange(256)
    t1 = np.arange(T1)
    angle = 2.0 * np.pi * (k1[:, None] * t1[None, :] % T1) / T1
    sine = -np.sin(angle)
    sine[0] = np.cos(np.pi * (t1 % 2))
    first = np.concatenate([np.cos(angle), sine], axis=0)
    t2 = np.arange(T2)
    turn = 2.0 * np.pi * (k1[:, None] * t2[None, :]) / TOTAL
    cos_t, sin_t = np.cos(turn), np.sin(turn)
    second = np.zeros((NB, 2, 4, 2, T2))
    edge = np.zeros((NB, 2, 4, 2, T2))
    for band in range(NB):
        for m, (k2, sign) in enumerate(
            [(2 * band, 1.0), (2 * band + 1, 1.0), (255 - 2 * band, -1.0), (254 - 2 * band, -1.0)]
        ):
            a = 2.0 * np.pi * (k2 * t2 % T2) / T2
            second[band, 0, m, 0] = np.cos(a)
            second[band, 0, m, 1] = np.sin(a)
            second[band, 1, m, 0] = -sign * np.sin(a)
            second[band, 1, m, 1] = sign * np.cos(a)
        for m in range(4):
            half = m // 2
            a = 2.0 * np.pi * ((2 * (2 * band + m % 2) + half) * t2 % 512) / 512
            edge[band, 0, m, half] = np.cos(a)
            edge[band, 1, m, half] = -np.sin(a)
    second = second.reshape(NB * 8, 2 * T2)
    edge = edge.reshape(NB * 8, 2 * T2)
    t = np.arange(TOTAL).reshape(T1, T2)
    window = 0.5 - 0.5 * np.cos(2.0 * np.pi * t / TOTAL)
    first_h, first_l = split_table(first)
    second_h, second_l = split_table(second)
    edge_h, edge_l = split_table(edge)
    return (
        window.astype(np.float32),
        cos_t.astype(np.float32),
        sin_t.astype(np.float32),
        first_h,
        first_l,
        second_h,
        second_l,
        edge_h,
        edge_l,
    )


def split(value):
    high = value.astype(jnp.bfloat16)
    low = (value - high.astype(jnp.float32)).astype(jnp.bfloat16)
    return high, low


def dot(a, b):
    return jnp.dot(a, b, preferred_element_type=jnp.float32)


def dot_nt(a, b):
    return lax.dot_general(a, b, NT, preferred_element_type=jnp.float32)


def pack_kernel(x_ref, o_ref, turned):
    for u in range(8):
        turned[u * 128 : (u + 1) * 128, :] = x_ref[0, u, 0].T
    for ch in range(CH):
        o_ref[ch % 64, ch // 64, 0, 0] = turned[pl.ds(ch, 8, stride=128), :]


def pack(samples):
    x = samples.reshape(2, 8, 2, 128, CH)
    return pl.pallas_call(
        pack_kernel,
        grid=(2, 2),
        in_specs=[pl.BlockSpec((1, 8, 1, 128, CH), lambda r, h: (r, 0, h, 0, 0))],
        out_specs=pl.BlockSpec((64, 2, 1, 1, 8, 128), lambda r, h: (0, 0, r, h, 0, 0)),
        out_shape=jax.ShapeDtypeStruct((64, 2, 2, 2, 8, 128), jnp.float32),
        scratch_shapes=[pltpu.VMEM((1024, 128), jnp.float32)],
        compiler_params=pltpu.CompilerParams(vmem_limit_bytes=16 * MIB),
        name="pack",
    )(x)


def dft_kernel(x_ref, w_ref, c_ref, s_ref, fh_ref, fl_ref, sh_ref, sl_ref, eh_ref, el_ref, o_ref):
    halves = [x_ref[:, 0, 0, h].reshape(T1, 128) for h in range(2)]
    x = jnp.concatenate(halves, axis=1) * w_ref[...]
    xh, xl = split(x)
    fh = fh_ref[...]
    a = dot(fh, xh) + dot(fh, xl) + dot(fl_ref[...], xh)
    a_re, a_im = a[:256], a[256:]
    c, s = c_ref[...], s_ref[...]
    b = jnp.concatenate([a_re * c + a_im * s, a_im * c - a_re * s], axis=1)
    first_row = lax.broadcasted_iota(jnp.int32, (256, 512), 0) == 0
    eh, el = split(jnp.where(first_row[:128], b[:128], 0.0))
    bh, bl = split(jnp.where(first_row, 0.0, b))
    sh = sh_ref[...]
    o = dot_nt(sh, bh) + dot_nt(sh, bl) + dot_nt(sl_ref[...], bh)
    edge = eh_ref[...]
    e = dot_nt(edge, eh) + dot_nt(edge, el) + dot_nt(el_ref[...], eh)
    o_ref[:, 0, 0] = (o[:, :128] + e).reshape(NB, 8, 128)
    o_ref[:, 0, 1] = o[:, 128:].reshape(NB, 8, 128)


def dft(x):
    consts = [jnp.asarray(t) for t in tables()]
    whole = [
        pl.BlockSpec(t.shape, lambda i: (0, 0), pipeline_mode=pl.Buffered(1)) for t in consts
    ]
    return pl.pallas_call(
        dft_kernel,
        grid=(4,),
        in_specs=[pl.BlockSpec((64, 1, 1, 2, 8, 128), lambda i: (0, i // 2, i % 2, 0, 0, 0))]
        + whole,
        out_specs=pl.BlockSpec((NB, 1, 2, 8, 128), lambda i: (0, i, 0, 0, 0)),
        out_shape=jax.ShapeDtypeStruct((NB, 4, 2, 8, 128), jnp.float32),
        compiler_params=pltpu.CompilerParams(vmem_limit_bytes=32 * MIB),
        name="dft",
    )(x, *consts)


def cross_kernel(x_ref, o_ref, *, scale):
    row = lax.broadcasted_iota(jnp.int32, (CH, CH), 0)
    col = lax.broadcasted_iota(jnp.int32, (CH, CH), 1)
    for r in range(2):
        parts = []
        for part in range(2):
            for c in range(2):
                cols = [
                    x_ref[pl.ds((c * 2 + r) * 16 + half * 8 + part * 4 + m, 64, stride=64), :]
                    for m in range(4)
                    for half in range(2)
                ]
                parts.append(jnp.concatenate(cols, axis=1))
        v = jnp.concatenate(parts, axis=0)
        vh, vl = split(v)
        mixed = dot_nt(vh, vl)
        g = dot_nt(vh, vh) + (mixed + mixed.T)
        real = g[:CH, :CH] + g[CH:, CH:]
        imag = g[CH:, :CH] - g[:CH, CH:]
        packed = jnp.where(row >= col, real, imag) * scale
        for y in range(8):
            o_ref[y, r] = packed


def cross(x):
    scale = 1.0 / (0.375 * BIN * TOTAL)
    return pl.pallas_call(
        functools.partial(cross_kernel, scale=scale),
        in_specs=[pl.BlockSpec(memory_space=pltpu.VMEM)],
        out_specs=pl.BlockSpec(memory_space=pltpu.VMEM),
        out_shape=jax.ShapeDtypeStruct((8, 2, CH, CH), jnp.float32),
        compiler_params=pltpu.CompilerParams(vmem_limit_bytes=32 * MIB),
        name="cross",
    )(x.reshape(64 * 64, 128))


def moments_kernel(lev_ref, roll_ref, x_ref, lm_ref, sp_ref, rm_ref, sums, rolls, squares):
    row = lax.broadcasted_iota(jnp.int32, (CH, CH), 0)
    col = lax.broadcasted_iota(jnp.int32, (CH, CH), 1)
    sums[...] = jnp.zeros_like(sums)
    rolls[...] = jnp.zeros_like(rolls)
    squares[...] = jnp.zeros_like(squares)

    def unpack(m):
        t = m.T
        real = jnp.where(row >= col, m, t)
        imag = jnp.where(row < col, m, jnp.where(row > col, -t, 0.0))
        return real, imag

    def count(ref, level):
        total = jnp.int32(0)
        for r in range(RUNS):
            total += (ref[r] == level).astype(jnp.int32)
        return jnp.maximum(total, 1).astype(jnp.float32)

    for r in range(RUNS):
        value = x_ref[r]
        sums[lev_ref[r]] += value
        rolls[roll_ref[r]] += value
    for l in range(NC):
        mean = sums[l] / count(lev_ref, l)
        sums[l] = mean
        real, imag = unpack(mean)
        lm_ref[l, 0, 0] = real
        lm_ref[l, 0, 1] = imag
    for q in range(NQ):
        real, imag = unpack(rolls[q] / count(roll_ref, q))
        rm_ref[q, 0, 0] = real
        rm_ref[q, 0, 1] = imag
    for r in range(RUNS):
        level = lev_ref[r]
        offset = x_ref[r] - sums[level]
        squares[level] += offset * offset
    for l in range(NC):
        s = squares[l]
        sp_ref[l, 0] = BIN * jnp.where(row == col, s, s + s.T)


def moments(cohesion, rolling, x):
    vmem = pl.BlockSpec(memory_space=pltpu.VMEM)
    smem = pl.BlockSpec(memory_space=pltpu.SMEM)
    return pl.pallas_call(
        moments_kernel,
        in_specs=[smem, smem, vmem],
        out_specs=(vmem, vmem, vmem),
        out_shape=(
            jax.ShapeDtypeStruct((NC, 1, 2, CH, CH), jnp.float32),
            jax.ShapeDtypeStruct((NC, 1, CH, CH), jnp.float32),
            jax.ShapeDtypeStruct((NQ, 1, 2, CH, CH), jnp.float32),
        ),
        scratch_shapes=[pltpu.VMEM((4, CH, CH), jnp.float32)] * 3,
        compiler_params=pltpu.CompilerParams(vmem_limit_bytes=16 * MIB),
        name="moments",
    )(cohesion, rolling, x.reshape(RUNS, CH, CH))


def exchange(x, axis):
    return lax.all_to_all(x, axis, split_axis=0, concat_axis=0, tiled=True)


def per_device(samples, cohesion, rolling):
    series = exchange(pack(samples).reshape(64, 64, 128), "tm")
    bins = dft(series.reshape(64, 2, 2, 2, 8, 128))
    band = exchange(bins.reshape(64, 64, 128), "tm")
    gathered = exchange(cross(band), "runs")
    return moments(cohesion, rolling, gathered)


def solution(mesh):
    return jax.shard_map(
        per_device,
        mesh=mesh,
        in_specs=(P("runs", "tm", None), P(), P()),
        out_specs=(
            P(None, "tm", None, None, None),
            P(None, "tm", None, None),
            P(None, "tm", None, None, None),
        ),
        check_vma=False,
    )
```

```python
import functools
import math

import jax
import jax.numpy as jnp
import ml_dtypes
import numpy as np
from jax import lax
from jax.experimental import pallas as pl
from jax.experimental.pallas import tpu as pltpu
from jax.sharding import PartitionSpec as P

CH = 128
BIN = 1024
NC = 4
NQ = 4
TOTAL = 131072
RUNS = 16
NB = 64
T1 = 512
T2 = 256

NT = (((1,), (1,)), ((), ()))
MIB = 1 << 20
STEP = 136


def split_table(table):
    high = table.astype(ml_dtypes.bfloat16)
    low = (table - high.astype(np.float64)).astype(ml_dtypes.bfloat16)
    return high, low


@functools.lru_cache(maxsize=None)
def tables():
    even, odd = np.arange(0, 256, 2), np.arange(1, 256, 2)
    t1 = np.arange(256)

    def trig(k, t, period):
        angle = 2.0 * np.pi * (k[:, None] * t[None, :] % period) / period
        return np.cos(angle), np.sin(angle)

    cos_e, sin_e = trig(even, t1, T1)
    cos_o, sin_o = trig(odd, t1, T1)
    sin_e[0] = -np.cos(np.pi * (t1 % 2))
    first_even = np.concatenate([cos_e, -sin_e], axis=0)
    first_odd = np.concatenate([cos_o, -sin_o], axis=0)
    t2 = np.arange(T2)
    cos_t, sin_t = trig(np.concatenate([even, odd]), t2, TOTAL)
    near = np.arange(128)
    second = np.zeros((2, NB, 2, 2, 2, 128))
    edge = np.zeros((NB, 8, T2))
    for band in range(NB):
        for parity in range(2):
            for m, (k2, sign) in enumerate(
                [(2 * band + parity, 1.0), (254 + parity - 2 * band, -1.0)]
            ):
                a = 2.0 * np.pi * (k2 * near % T2) / T2
                second[parity, band, 0, m, 0] = np.cos(a)
                second[parity, band, 0, m, 1] = np.sin(a)
                second[parity, band, 1, m, 0] = -sign * np.sin(a)
                second[parity, band, 1, m, 1] = sign * np.cos(a)
        for half in range(2):
            for m in range(2):
                a = 2.0 * np.pi * ((2 * (2 * band + m) + half) * t2 % 512) / 512
                edge[band, 4 * half + m] = np.cos(a)
                edge[band, 4 * half + 2 + m] = -np.sin(a)
    t = np.arange(TOTAL).reshape(T1, T2)
    window = 0.5 - 0.5 * np.cos(2.0 * np.pi * t / TOTAL)

    def passes(table):
        high, low = split_table(table)
        return np.concatenate([high, high, low], axis=1)

    return (
        window.astype(np.float32),
        cos_t.astype(np.float32),
        sin_t.astype(np.float32),
        passes(first_even),
        passes(first_odd),
        passes(second[0].reshape(256, 256)),
        passes(second[1].reshape(256, 256)),
        passes(edge.reshape(NB * 8, T2)),
    )


def split(value):
    high = value.astype(jnp.bfloat16)
    low = (value - high.astype(jnp.float32)).astype(jnp.bfloat16)
    return high, low


def dot(a, b):
    return jnp.dot(a, b, preferred_element_type=jnp.float32)


def dot_nt(a, b):
    return lax.dot_general(a, b, NT, preferred_element_type=jnp.float32)


def pack_kernel(x_hbm, o_ref, landed, turned, sems):
    copies = [
        pltpu.make_async_copy(x_hbm.at[r, :, h], landed.at[r, h], sems.at[r, h])
        for r in range(2)
        for h in range(2)
    ]
    for copy in copies:
        copy.start()
    for r in range(2):
        for h in range(2):
            copies[2 * r + h].wait()
            for u in range(8):
                turned[r, h, u * STEP : u * STEP + 128, :] = landed[r, h, u].T
            for ch in range(CH):
                o_ref[ch % 64, ch // 64, r, h] = turned[r, h, pl.ds(ch, 8, stride=STEP), :]


def pack(samples):
    x = samples.reshape(2, 8, 2, 128, CH)
    return pl.pallas_call(
        pack_kernel,
        in_specs=[pl.BlockSpec(memory_space=pltpu.HBM)],
        out_specs=pl.BlockSpec(memory_space=pltpu.VMEM),
        out_shape=jax.ShapeDtypeStruct((64, 2, 2, 2, 8, 128), jnp.float32),
        scratch_shapes=[
            pltpu.VMEM((2, 2, 8, 128, CH), jnp.float32),
            pltpu.VMEM((2, 2, 8 * STEP, 128), jnp.float32),
            pltpu.SemaphoreType.DMA((2, 2)),
        ],
        compiler_params=pltpu.CompilerParams(vmem_limit_bytes=50 * MIB),
        name="pack",
    )(x)


def dft_kernel(
    x_ref, w_ref, c_ref, s_ref, fe_ref, fo_ref, se_ref, so_ref, edge_ref, o_ref, edge_in
):
    edge_in[...] = jnp.zeros_like(edge_in)
    first_row = lax.broadcasted_iota(jnp.int32, (256, T2), 0) == 0
    upper = lax.broadcasted_iota(jnp.int32, (32, 8, 128), 1) < 4

    @pl.loop(0, 4)
    def _(i):
        halves = [x_ref[:, i // 2, i % 2, h].reshape(T1, 128) for h in range(2)]
        x = jnp.concatenate(halves, axis=1) * w_ref[...]
        xh, xl = split(x[:256] + x[256:])
        a_even = dot(fe_ref[...], jnp.concatenate([xh, xl, xh], axis=0))
        xh, xl = split(x[:256] - x[256:])
        a_odd = dot(fo_ref[...], jnp.concatenate([xh, xl, xh], axis=0))
        a_re = jnp.concatenate([a_even[:128], a_odd[:128]], axis=0)
        a_im = jnp.concatenate([a_even[128:], a_odd[128:]], axis=0)
        c, s = c_ref[...], s_ref[...]
        b_re = a_re * c + a_im * s
        b_im = a_im * c - a_re * s
        edge_in[pl.ds(i, 1), :] = b_re[:1]
        edge_in[pl.ds(i + 4, 1), :] = b_im[:1]
        b_re = jnp.where(first_row, 0.0, b_re)
        b_im = jnp.where(first_row, 0.0, b_im)
        plus = jnp.concatenate(
            [b_re[:, :128] + b_re[:, 128:], b_im[:, :128] + b_im[:, 128:]], axis=1
        )
        minus = jnp.concatenate(
            [b_re[:, :128] - b_re[:, 128:], b_im[:, :128] - b_im[:, 128:]], axis=1
        )
        bh, bl = split(plus)
        o_even = dot_nt(se_ref[...], jnp.concatenate([bh, bl, bh], axis=1))
        bh, bl = split(minus)
        o_odd = dot_nt(so_ref[...], jnp.concatenate([bh, bl, bh], axis=1))
        for half in range(2):
            lanes = slice(128 * half, 128 * half + 128)
            e = o_even[:, lanes].reshape(32, 8, 128)
            o = o_odd[:, lanes].reshape(32, 8, 128)
            o_ref[:, 0, i, half] = jnp.where(upper, e, pltpu.roll(o, 4, 1))
            o_ref[:, 1, i, half] = jnp.where(upper, pltpu.roll(e, 4, 1), o)

    eh, el = split(edge_in[...])
    e = dot_nt(edge_ref[...], jnp.concatenate([eh, el, eh], axis=1))
    first_lane = lax.broadcasted_iota(jnp.int32, (512, 128), 1) == 0
    sub = lax.broadcasted_iota(jnp.int32, (512, 128), 0) % 8 < 4
    for i in range(4):
        low = e if i == 0 else pltpu.roll(e, 128 - i, 1)
        value = jnp.where(sub, low, pltpu.roll(e, 124 - i, 1))
        o_ref[:, :, i, 0] += jnp.where(first_lane, value, 0.0).reshape(32, 2, 8, 128)


def dft(x):
    consts = [jnp.asarray(t) for t in tables()]
    vmem = pl.BlockSpec(memory_space=pltpu.VMEM)
    return pl.pallas_call(
        dft_kernel,
        in_specs=[vmem] * (1 + len(consts)),
        out_specs=vmem,
        out_shape=jax.ShapeDtypeStruct((NB // 2, 2, 4, 2, 8, 128), jnp.float32),
        scratch_shapes=[pltpu.VMEM((128, T2), jnp.float32)],
        compiler_params=pltpu.CompilerParams(vmem_limit_bytes=24 * MIB),
        name="dft",
    )(x, *consts)


def cross_kernel(x_ref, o_ref, *, scale):
    row = lax.broadcasted_iota(jnp.int32, (CH, CH), 0)
    col = lax.broadcasted_iota(jnp.int32, (CH, CH), 1)
    for r in range(2):
        parts = []
        for part in range(2):
            for c in range(2):
                cols = [
                    x_ref[pl.ds((c * 2 + r) * 16 + half * 8 + part * 2 + m, 64, stride=64), :]
                    for m in (0, 1, 4, 5)
                    for half in range(2)
                ]
                parts.append(jnp.concatenate(cols, axis=1))
        v = jnp.concatenate(parts, axis=0)
        vh, vl = split(v)
        mixed = dot_nt(vh, vl)
        g = dot_nt(vh, vh) + (mixed + mixed.T)
        real = g[:CH, :CH] + g[CH:, CH:]
        imag = g[CH:, :CH] - g[:CH, CH:]
        packed = jnp.where(row >= col, real, imag) * scale
        for y in range(8):
            o_ref[y, r] = packed


def cross(x):
    scale = 1.0 / (0.375 * BIN * TOTAL)
    return pl.pallas_call(
        functools.partial(cross_kernel, scale=scale),
        in_specs=[pl.BlockSpec(memory_space=pltpu.VMEM)],
        out_specs=pl.BlockSpec(memory_space=pltpu.VMEM),
        out_shape=jax.ShapeDtypeStruct((8, 2, CH, CH), jnp.float32),
        compiler_params=pltpu.CompilerParams(vmem_limit_bytes=24 * MIB),
        name="cross",
    )(x.reshape(64 * 64, 128))


def moments_kernel(
    lev_ref, roll_ref, x_ref, lm_hbm, sp_hbm, rm_hbm, sums, rolls, squares, lm, sp, rm, sems
):
    row = lax.broadcasted_iota(jnp.int32, (CH, CH), 0)
    col = lax.broadcasted_iota(jnp.int32, (CH, CH), 1)
    sums[...] = jnp.zeros_like(sums)
    rolls[...] = jnp.zeros_like(rolls)
    squares[...] = jnp.zeros_like(squares)

    def unpack(m):
        t = m.T
        real = jnp.where(row >= col, m, t)
        imag = jnp.where(row < col, m, jnp.where(row > col, -t, 0.0))
        return real, imag

    def count(ref, level):
        total = jnp.int32(0)
        for r in range(RUNS):
            total += (ref[r] == level).astype(jnp.int32)
        return jnp.maximum(total, 1).astype(jnp.float32)

    for r in range(RUNS):
        rolls[roll_ref[r]] += x_ref[r]
    for q in range(NQ):
        rm[q, 0, 0], rm[q, 0, 1] = unpack(rolls[q] / count(roll_ref, q))
    send_rm = pltpu.make_async_copy(rm, rm_hbm, sems.at[0])
    send_rm.start()
    for r in range(RUNS):
        sums[lev_ref[r]] += x_ref[r]
    for l in range(NC):
        mean = sums[l] / count(lev_ref, l)
        sums[l] = mean
        lm[l, 0, 0], lm[l, 0, 1] = unpack(mean)
    send_lm = pltpu.make_async_copy(lm, lm_hbm, sems.at[1])
    send_lm.start()
    for r in range(RUNS):
        level = lev_ref[r]
        offset = x_ref[r] - sums[level]
        squares[level] += offset * offset
    for l in range(NC):
        s = squares[l]
        sp[l, 0] = BIN * jnp.where(row == col, s, s + s.T)
    send_sp = pltpu.make_async_copy(sp, sp_hbm, sems.at[2])
    send_sp.start()
    send_rm.wait()
    send_lm.wait()
    send_sp.wait()


def moments(cohesion, rolling, x):
    vmem = pl.BlockSpec(memory_space=pltpu.VMEM)
    smem = pl.BlockSpec(memory_space=pltpu.SMEM)
    hbm = pl.BlockSpec(memory_space=pltpu.HBM)
    shapes = [(NC, 1, 2, CH, CH), (NC, 1, CH, CH), (NQ, 1, 2, CH, CH)]
    return pl.pallas_call(
        moments_kernel,
        in_specs=[smem, smem, vmem],
        out_specs=(hbm, hbm, hbm),
        out_shape=tuple(jax.ShapeDtypeStruct(shape, jnp.float32) for shape in shapes),
        scratch_shapes=[pltpu.VMEM((4, CH, CH), jnp.float32)] * 3
        + [pltpu.VMEM(shape, jnp.float32) for shape in shapes]
        + [pltpu.SemaphoreType.DMA((3,))],
        compiler_params=pltpu.CompilerParams(vmem_limit_bytes=16 * MIB),
        name="moments",
    )(cohesion, rolling, x.reshape(RUNS, CH, CH))


def exchange(x, axis):
    return lax.all_to_all(x, axis, split_axis=0, concat_axis=0, tiled=True)


def per_device(samples, cohesion, rolling):
    series = exchange(pack(samples).reshape(64, 64, 128), "tm")
    bins = dft(series.reshape(64, 2, 2, 2, 8, 128))
    band = exchange(bins.reshape(64, 64, 128), "tm")
    gathered = exchange(cross(band), "runs")
    return moments(cohesion, rolling, gathered)


def solution(mesh):
    return jax.shard_map(
        per_device,
        mesh=mesh,
        in_specs=(P("runs", "tm", None), P(), P()),
        out_specs=(
            P(None, "tm", None, None, None),
            P(None, "tm", None, None),
            P(None, "tm", None, None, None),
        ),
        check_vma=False,
    )
```

```python
import functools
import math

import jax
import jax.numpy as jnp
import ml_dtypes
import numpy as np
from jax import lax
from jax.experimental import pallas as pl
from jax.experimental.pallas import tpu as pltpu
from jax.sharding import PartitionSpec as P

CH = 128
BIN = 1024
NC = 4
NQ = 4
TOTAL = 131072
RUNS = 16
NB = 64
T1 = 512
T2 = 256

NT = (((1,), (1,)), ((), ()))
MIB = 1 << 20
PITCH = 72
STEP = 136


def split_table(table):
    high = table.astype(ml_dtypes.bfloat16)
    low = (table - high.astype(np.float64)).astype(ml_dtypes.bfloat16)
    return high, low


@functools.lru_cache(maxsize=None)
def tables():
    even, odd = np.arange(0, 256, 2), np.arange(1, 256, 2)
    t1 = np.arange(256)

    def trig(k, t, period):
        angle = 2.0 * np.pi * (k[:, None] * t[None, :] % period) / period
        return np.cos(angle), np.sin(angle)

    cos_e, sin_e = trig(even, t1, T1)
    cos_o, sin_o = trig(odd, t1, T1)
    sin_e[0] = -np.cos(np.pi * (t1 % 2))
    first_even = np.concatenate([cos_e, -sin_e], axis=0)
    first_odd = np.concatenate([cos_o, -sin_o], axis=0)
    t2 = np.arange(T2)
    cos_t, sin_t = trig(np.concatenate([even, odd]), t2, TOTAL)
    near = np.arange(128)
    second = np.zeros((2, NB, 2, 2, 2, 128))
    edge = np.zeros((NB, 8, T2))
    for band in range(NB):
        for parity in range(2):
            for m, (k2, sign) in enumerate(
                [(2 * band + parity, 1.0), (254 + parity - 2 * band, -1.0)]
            ):
                a = 2.0 * np.pi * (k2 * near % T2) / T2
                second[parity, band, 0, m, 0] = np.cos(a)
                second[parity, band, 0, m, 1] = np.sin(a)
                second[parity, band, 1, m, 0] = -sign * np.sin(a)
                second[parity, band, 1, m, 1] = sign * np.cos(a)
        for half in range(2):
            for m in range(2):
                a = 2.0 * np.pi * ((2 * (2 * band + m) + half) * t2 % 512) / 512
                edge[band, 4 * half + m] = np.cos(a)
                edge[band, 4 * half + 2 + m] = -np.sin(a)
    t = np.arange(TOTAL).reshape(T1, T2)
    window = 0.5 - 0.5 * np.cos(2.0 * np.pi * t / TOTAL)

    def passes(table):
        high, low = split_table(table)
        return np.concatenate([high, high, low], axis=1)

    return (
        window.astype(np.float32),
        cos_t.astype(np.float32),
        sin_t.astype(np.float32),
        passes(first_even),
        passes(first_odd),
        passes(second[0].reshape(256, 256)),
        passes(second[1].reshape(256, 256)),
        passes(edge.reshape(NB * 8, T2)),
    )


def split(value):
    high = value.astype(jnp.bfloat16)
    low = (value - high.astype(jnp.float32)).astype(jnp.bfloat16)
    return high, low


def dot(a, b):
    return jnp.dot(a, b, preferred_element_type=jnp.float32)


def dot_nt(a, b):
    return lax.dot_general(a, b, NT, preferred_element_type=jnp.float32)


def pack_kernel(x_hbm, o_ref, landed, turned, sems):
    copies = [
        pltpu.make_async_copy(x_hbm.at[r, :, h], landed.at[r, h], sems.at[r, h])
        for r in range(2)
        for h in range(2)
    ]
    for copy in copies:
        copy.start()
    for r in range(2):
        for h in range(2):
            copies[2 * r + h].wait()
            for u in range(8):
                turned[r, h, u * STEP : u * STEP + 128, :] = landed[r, h, u].T
            for ch in range(CH):
                o_ref[ch % 64, ch // 64, r, h] = turned[r, h, pl.ds(ch, 8, stride=STEP), :]


def pack(samples):
    x = samples.reshape(2, 8, 2, 128, CH)
    return pl.pallas_call(
        pack_kernel,
        in_specs=[pl.BlockSpec(memory_space=pltpu.HBM)],
        out_specs=pl.BlockSpec(memory_space=pltpu.VMEM),
        out_shape=jax.ShapeDtypeStruct((64, 2, 2, 2, 8, 128), jnp.float32),
        scratch_shapes=[
            pltpu.VMEM((2, 2, 8, 128, CH), jnp.float32),
            pltpu.VMEM((2, 2, 8 * STEP, 128), jnp.float32),
            pltpu.SemaphoreType.DMA((2, 2)),
        ],
        compiler_params=pltpu.CompilerParams(vmem_limit_bytes=50 * MIB),
        name="pack",
    )(x)


def dft_kernel(
    x_ref, w_ref, c_ref, s_ref, fe_ref, fo_ref, se_ref, so_ref, edge_ref, o_ref, edge_in
):
    edge_in[...] = jnp.zeros_like(edge_in)
    first_row = lax.broadcasted_iota(jnp.int32, (256, T2), 0) == 0
    upper = lax.broadcasted_iota(jnp.int32, (32, 8, 128), 1) < 4

    @pl.loop(0, 4, unroll=4)
    def _(i):
        halves = [x_ref[:, i // 2, i % 2, h].reshape(T1, 128) for h in range(2)]
        x = jnp.concatenate(halves, axis=1) * w_ref[...]
        xh, xl = split(x[:256] + x[256:])
        a_even = dot(fe_ref[...], jnp.concatenate([xh, xl, xh], axis=0))
        xh, xl = split(x[:256] - x[256:])
        a_odd = dot(fo_ref[...], jnp.concatenate([xh, xl, xh], axis=0))
        a_re = jnp.concatenate([a_even[:128], a_odd[:128]], axis=0)
        a_im = jnp.concatenate([a_even[128:], a_odd[128:]], axis=0)
        c, s = c_ref[...], s_ref[...]
        b_re = a_re * c + a_im * s
        b_im = a_im * c - a_re * s
        edge_in[pl.ds(i, 1), :] = b_re[:1]
        edge_in[pl.ds(i + 4, 1), :] = b_im[:1]
        b_re = jnp.where(first_row, 0.0, b_re)
        b_im = jnp.where(first_row, 0.0, b_im)
        plus = jnp.concatenate(
            [b_re[:, :128] + b_re[:, 128:], b_im[:, :128] + b_im[:, 128:]], axis=1
        )
        minus = jnp.concatenate(
            [b_re[:, :128] - b_re[:, 128:], b_im[:, :128] - b_im[:, 128:]], axis=1
        )
        bh, bl = split(plus)
        o_even = dot_nt(se_ref[...], jnp.concatenate([bh, bl, bh], axis=1))
        bh, bl = split(minus)
        o_odd = dot_nt(so_ref[...], jnp.concatenate([bh, bl, bh], axis=1))
        for half in range(2):
            lanes = slice(128 * half, 128 * half + 128)
            e = o_even[:, lanes].reshape(32, 8, 128)
            o = o_odd[:, lanes].reshape(32, 8, 128)
            o_ref[:, 0, i, half] = jnp.where(upper, e, pltpu.roll(o, 4, 1))
            o_ref[:, 1, i, half] = jnp.where(upper, pltpu.roll(e, 4, 1), o)

    eh, el = split(edge_in[...])
    e = dot_nt(edge_ref[...], jnp.concatenate([eh, el, eh], axis=1))
    first_lane = lax.broadcasted_iota(jnp.int32, (512, 128), 1) == 0
    sub = lax.broadcasted_iota(jnp.int32, (512, 128), 0) % 8 < 4
    for i in range(4):
        low = e if i == 0 else pltpu.roll(e, 128 - i, 1)
        value = jnp.where(sub, low, pltpu.roll(e, 124 - i, 1))
        o_ref[:, :, i, 0] += jnp.where(first_lane, value, 0.0).reshape(32, 2, 8, 128)


def dft(x):
    consts = [jnp.asarray(t) for t in tables()]
    vmem = pl.BlockSpec(memory_space=pltpu.VMEM)
    return pl.pallas_call(
        dft_kernel,
        in_specs=[vmem] * (1 + len(consts)),
        out_specs=vmem,
        out_shape=jax.ShapeDtypeStruct((NB // 2, 2, 4, 2, 8, 128), jnp.float32),
        scratch_shapes=[pltpu.VMEM((128, T2), jnp.float32)],
        compiler_params=pltpu.CompilerParams(vmem_limit_bytes=24 * MIB),
        name="dft",
    )(x, *consts)


def cross_kernel(x_ref, o_ref, rows, *, scale):
    row = lax.broadcasted_iota(jnp.int32, (CH, CH), 0)
    col = lax.broadcasted_iota(jnp.int32, (CH, CH), 1)
    for q in range(64):
        rows[q * PITCH : q * PITCH + 64, :] = x_ref[q * 64 : q * 64 + 64, :]
    for r in range(2):
        parts = []
        for part in range(2):
            for c in range(2):
                cols = [
                    rows[pl.ds((c * 2 + r) * 16 + half * 8 + part * 2 + m, 64, stride=PITCH), :]
                    for m in (0, 1, 4, 5)
                    for half in range(2)
                ]
                parts.append(jnp.concatenate(cols, axis=1))
        v = jnp.concatenate(parts, axis=0)
        vh, vl = split(v)
        mixed = dot_nt(vh, vl)
        g = dot_nt(vh, vh) + (mixed + mixed.T)
        real = g[:CH, :CH] + g[CH:, CH:]
        imag = g[CH:, :CH] - g[:CH, CH:]
        packed = jnp.where(row >= col, real, imag) * scale
        for y in range(8):
            o_ref[y, r] = packed


def cross(x):
    scale = 1.0 / (0.375 * BIN * TOTAL)
    return pl.pallas_call(
        functools.partial(cross_kernel, scale=scale),
        in_specs=[pl.BlockSpec(memory_space=pltpu.VMEM)],
        out_specs=pl.BlockSpec(memory_space=pltpu.VMEM),
        out_shape=jax.ShapeDtypeStruct((8, 2, CH, CH), jnp.float32),
        scratch_shapes=[pltpu.VMEM((64 * PITCH, 128), jnp.float32)],
        compiler_params=pltpu.CompilerParams(vmem_limit_bytes=24 * MIB),
        name="cross",
    )(x.reshape(64 * 64, 128))


def moments_kernel(
    lev_ref, roll_ref, x_ref, lm_hbm, sp_hbm, rm_hbm, sums, rolls, squares, lm, sp, rm, sems
):
    row = lax.broadcasted_iota(jnp.int32, (CH, CH), 0)
    col = lax.broadcasted_iota(jnp.int32, (CH, CH), 1)
    sums[...] = jnp.zeros_like(sums)
    rolls[...] = jnp.zeros_like(rolls)
    squares[...] = jnp.zeros_like(squares)

    def unpack(m):
        t = m.T
        real = jnp.where(row >= col, m, t)
        imag = jnp.where(row < col, m, jnp.where(row > col, -t, 0.0))
        return real, imag

    def count(ref, level):
        total = jnp.int32(0)
        for r in range(RUNS):
            total += (ref[r] == level).astype(jnp.int32)
        return jnp.maximum(total, 1).astype(jnp.float32)

    for r in range(RUNS):
        rolls[roll_ref[r]] += x_ref[r]
    for q in range(NQ):
        rm[q, 0, 0], rm[q, 0, 1] = unpack(rolls[q] / count(roll_ref, q))
    send_rm = pltpu.make_async_copy(rm, rm_hbm, sems.at[0])
    send_rm.start()
    for r in range(RUNS):
        sums[lev_ref[r]] += x_ref[r]
    for l in range(NC):
        mean = sums[l] / count(lev_ref, l)
        sums[l] = mean
        lm[l, 0, 0], lm[l, 0, 1] = unpack(mean)
    send_lm = pltpu.make_async_copy(lm, lm_hbm, sems.at[1])
    send_lm.start()
    for r in range(RUNS):
        level = lev_ref[r]
        offset = x_ref[r] - sums[level]
        squares[level] += offset * offset
    for l in range(NC):
        s = squares[l]
        sp[l, 0] = BIN * jnp.where(row == col, s, s + s.T)
    send_sp = pltpu.make_async_copy(sp, sp_hbm, sems.at[2])
    send_sp.start()
    send_rm.wait()
    send_lm.wait()
    send_sp.wait()


def moments(cohesion, rolling, x):
    vmem = pl.BlockSpec(memory_space=pltpu.VMEM)
    smem = pl.BlockSpec(memory_space=pltpu.SMEM)
    hbm = pl.BlockSpec(memory_space=pltpu.HBM)
    shapes = [(NC, 1, 2, CH, CH), (NC, 1, CH, CH), (NQ, 1, 2, CH, CH)]
    return pl.pallas_call(
        moments_kernel,
        in_specs=[smem, smem, vmem],
        out_specs=(hbm, hbm, hbm),
        out_shape=tuple(jax.ShapeDtypeStruct(shape, jnp.float32) for shape in shapes),
        scratch_shapes=[pltpu.VMEM((4, CH, CH), jnp.float32)] * 3
        + [pltpu.VMEM(shape, jnp.float32) for shape in shapes]
        + [pltpu.SemaphoreType.DMA((3,))],
        compiler_params=pltpu.CompilerParams(vmem_limit_bytes=16 * MIB),
        name="moments",
    )(cohesion, rolling, x.reshape(RUNS, CH, CH))


def exchange(x, axis):
    return lax.all_to_all(x, axis, split_axis=0, concat_axis=0, tiled=True)


def per_device(samples, cohesion, rolling):
    series = exchange(pack(samples).reshape(64, 64, 128), "tm")
    bins = dft(series.reshape(64, 2, 2, 2, 8, 128))
    band = exchange(bins.reshape(64, 64, 128), "tm")
    gathered = exchange(cross(band), "runs")
    return moments(cohesion, rolling, gathered)


def solution(mesh):
    return jax.shard_map(
        per_device,
        mesh=mesh,
        in_specs=(P("runs", "tm", None), P(), P()),
        out_specs=(
            P(None, "tm", None, None, None),
            P(None, "tm", None, None),
            P(None, "tm", None, None, None),
        ),
        check_vma=False,
    )
```

```python
import functools
import math

import jax
import jax.numpy as jnp
import ml_dtypes
import numpy as np
from jax import lax
from jax.experimental import pallas as pl
from jax.experimental.pallas import tpu as pltpu
from jax.sharding import PartitionSpec as P

CH = 128
BIN = 1024
NC = 4
NQ = 4
TOTAL = 131072
RUNS = 16
NB = 64
T1 = 512
T2 = 256

NT = (((1,), (1,)), ((), ()))
MIB = 1 << 20
PITCH = 72
STEP = 136


def split_table(table):
    high = table.astype(ml_dtypes.bfloat16)
    low = (table - high.astype(np.float64)).astype(ml_dtypes.bfloat16)
    return high, low


@functools.lru_cache(maxsize=None)
def tables():
    even, odd = np.arange(0, 256, 2), np.arange(1, 256, 2)
    t1 = np.arange(256)

    def trig(k, t, period):
        angle = 2.0 * np.pi * (k[:, None] * t[None, :] % period) / period
        return np.cos(angle), np.sin(angle)

    cos_e, sin_e = trig(even, t1, T1)
    cos_o, sin_o = trig(odd, t1, T1)
    sin_e[0] = -np.cos(np.pi * (t1 % 2))
    first_even = np.concatenate([cos_e, -sin_e], axis=0)
    first_odd = np.concatenate([cos_o, -sin_o], axis=0)
    t2 = np.arange(T2)
    cos_t, sin_t = trig(np.concatenate([even, odd]), t2, TOTAL)
    near = np.arange(128)
    second = np.zeros((2, NB, 2, 2, 2, 128))
    edge = np.zeros((NB, 8, T2))
    for band in range(NB):
        for parity in range(2):
            for m, (k2, sign) in enumerate(
                [(2 * band + parity, 1.0), (254 + parity - 2 * band, -1.0)]
            ):
                a = 2.0 * np.pi * (k2 * near % T2) / T2
                second[parity, band, 0, m, 0] = np.cos(a)
                second[parity, band, 0, m, 1] = np.sin(a)
                second[parity, band, 1, m, 0] = -sign * np.sin(a)
                second[parity, band, 1, m, 1] = sign * np.cos(a)
        for half in range(2):
            for m in range(2):
                a = 2.0 * np.pi * ((2 * (2 * band + m) + half) * t2 % 512) / 512
                edge[band, 4 * half + m] = np.cos(a)
                edge[band, 4 * half + 2 + m] = -np.sin(a)
    t = np.arange(TOTAL).reshape(T1, T2)
    window = 0.5 - 0.5 * np.cos(2.0 * np.pi * t / TOTAL)

    def passes(table):
        high, low = split_table(table)
        return np.concatenate([high, high, low], axis=1)

    return (
        window.astype(np.float32),
        cos_t.astype(np.float32),
        sin_t.astype(np.float32),
        passes(first_even),
        passes(first_odd),
        passes(second[0].reshape(256, 256)),
        passes(second[1].reshape(256, 256)),
        passes(edge.reshape(NB * 8, T2)),
    )


def split(value):
    high = value.astype(jnp.bfloat16)
    low = (value - high.astype(jnp.float32)).astype(jnp.bfloat16)
    return high, low


def dot(a, b):
    return jnp.dot(a, b, preferred_element_type=jnp.float32)


def dot_nt(a, b):
    return lax.dot_general(a, b, NT, preferred_element_type=jnp.float32)


def pack_kernel(x_hbm, o_ref, landed, turned, sems):
    copies = [
        pltpu.make_async_copy(x_hbm.at[r, :, h], landed.at[r, h], sems.at[r, h])
        for r in range(2)
        for h in range(2)
    ]
    for copy in copies:
        copy.start()
    for r in range(2):
        for h in range(2):
            copies[2 * r + h].wait()
            for u in range(8):
                turned[r, h, u * STEP : u * STEP + 128, :] = landed[r, h, u].T
            for ch in range(CH):
                o_ref[ch % 64, ch // 64, r, h] = turned[r, h, pl.ds(ch, 8, stride=STEP), :]


def pack(samples):
    x = samples.reshape(2, 8, 2, 128, CH)
    return pl.pallas_call(
        pack_kernel,
        in_specs=[pl.BlockSpec(memory_space=pltpu.HBM)],
        out_specs=pl.BlockSpec(memory_space=pltpu.VMEM),
        out_shape=jax.ShapeDtypeStruct((64, 2, 2, 2, 8, 128), jnp.float32),
        scratch_shapes=[
            pltpu.VMEM((2, 2, 8, 128, CH), jnp.float32),
            pltpu.VMEM((2, 2, 8 * STEP, 128), jnp.float32),
            pltpu.SemaphoreType.DMA((2, 2)),
        ],
        compiler_params=pltpu.CompilerParams(vmem_limit_bytes=50 * MIB),
        name="pack",
    )(x)


def dft_kernel(
    x_ref, w_ref, c_ref, s_ref, fe_ref, fo_ref, se_ref, so_ref, edge_ref, o_ref, edge_in, middle
):
    edge_in[...] = jnp.zeros_like(edge_in)
    first_row = lax.broadcasted_iota(jnp.int32, (256, T2), 0) == 0
    upper = lax.broadcasted_iota(jnp.int32, (32, 8, 128), 1) < 4

    for i in range(4):
        halves = [x_ref[:, i // 2, i % 2, h].reshape(T1, 128) for h in range(2)]
        x = jnp.concatenate(halves, axis=1) * w_ref[...]
        xh, xl = split(x[:256] + x[256:])
        a_even = dot(fe_ref[...], jnp.concatenate([xh, xl, xh], axis=0))
        xh, xl = split(x[:256] - x[256:])
        a_odd = dot(fo_ref[...], jnp.concatenate([xh, xl, xh], axis=0))
        a_re = jnp.concatenate([a_even[:128], a_odd[:128]], axis=0)
        a_im = jnp.concatenate([a_even[128:], a_odd[128:]], axis=0)
        c, s = c_ref[...], s_ref[...]
        b_re = a_re * c + a_im * s
        b_im = a_im * c - a_re * s
        edge_in[i : i + 1, :] = b_re[:1]
        edge_in[i + 4 : i + 5, :] = b_im[:1]
        b_re = jnp.where(first_row, 0.0, b_re)
        b_im = jnp.where(first_row, 0.0, b_im)
        plus = jnp.concatenate(
            [b_re[:, :128] + b_re[:, 128:], b_im[:, :128] + b_im[:, 128:]], axis=1
        )
        minus = jnp.concatenate(
            [b_re[:, :128] - b_re[:, 128:], b_im[:, :128] - b_im[:, 128:]], axis=1
        )
        middle[i, 0, 0], middle[i, 0, 1] = split(plus)
        middle[i, 1, 0], middle[i, 1, 1] = split(minus)

    eh, el = split(edge_in[...])
    edge = dot_nt(edge_ref[...], jnp.concatenate([eh, el, eh], axis=1))
    first_lane = lax.broadcasted_iota(jnp.int32, (512, 128), 1) == 0
    sub = lax.broadcasted_iota(jnp.int32, (512, 128), 0) % 8 < 4

    for i in range(4):
        bh, bl = middle[i, 0, 0], middle[i, 0, 1]
        o_even = dot_nt(se_ref[...], jnp.concatenate([bh, bl, bh], axis=1))
        bh, bl = middle[i, 1, 0], middle[i, 1, 1]
        o_odd = dot_nt(so_ref[...], jnp.concatenate([bh, bl, bh], axis=1))
        low = edge if i == 0 else pltpu.roll(edge, 128 - i, 1)
        extra = jnp.where(sub, low, pltpu.roll(edge, 124 - i, 1))
        extra = jnp.where(first_lane, extra, 0.0).reshape(32, 2, 8, 128)
        for half in range(2):
            lanes = slice(128 * half, 128 * half + 128)
            e = o_even[:, lanes].reshape(32, 8, 128)
            o = o_odd[:, lanes].reshape(32, 8, 128)
            first = jnp.where(upper, e, pltpu.roll(o, 4, 1))
            second = jnp.where(upper, pltpu.roll(e, 4, 1), o)
            o_ref[:, 0, i, half] = first + extra[:, 0] if half == 0 else first
            o_ref[:, 1, i, half] = second + extra[:, 1] if half == 0 else second


def dft(x):
    consts = [jnp.asarray(t) for t in tables()]
    vmem = pl.BlockSpec(memory_space=pltpu.VMEM)
    return pl.pallas_call(
        dft_kernel,
        in_specs=[vmem] * (1 + len(consts)),
        out_specs=vmem,
        out_shape=jax.ShapeDtypeStruct((NB // 2, 2, 4, 2, 8, 128), jnp.float32),
        scratch_shapes=[
            pltpu.VMEM((128, T2), jnp.float32),
            pltpu.VMEM((4, 2, 2, 256, 256), jnp.bfloat16),
        ],
        compiler_params=pltpu.CompilerParams(vmem_limit_bytes=24 * MIB),
        name="dft",
    )(x, *consts)


def cross_kernel(x_ref, o_ref, rows, *, scale):
    row = lax.broadcasted_iota(jnp.int32, (CH, CH), 0)
    col = lax.broadcasted_iota(jnp.int32, (CH, CH), 1)
    for q in range(64):
        rows[q * PITCH : q * PITCH + 64, :] = x_ref[q * 64 : q * 64 + 64, :]
    for r in range(2):
        parts = []
        for part in range(2):
            for c in range(2):
                cols = [
                    rows[pl.ds((c * 2 + r) * 16 + half * 8 + part * 2 + m, 64, stride=PITCH), :]
                    for m in (0, 1, 4, 5)
                    for half in range(2)
                ]
                parts.append(jnp.concatenate(cols, axis=1))
        v = jnp.concatenate(parts, axis=0)
        vh, vl = split(v)
        mixed = dot_nt(vh, vl)
        g = dot_nt(vh, vh) + (mixed + mixed.T)
        real = g[:CH, :CH] + g[CH:, CH:]
        imag = g[CH:, :CH] - g[:CH, CH:]
        packed = jnp.where(row >= col, real, imag) * scale
        for y in range(8):
            o_ref[y, r] = packed


def cross(x):
    scale = 1.0 / (0.375 * BIN * TOTAL)
    return pl.pallas_call(
        functools.partial(cross_kernel, scale=scale),
        in_specs=[pl.BlockSpec(memory_space=pltpu.VMEM)],
        out_specs=pl.BlockSpec(memory_space=pltpu.VMEM),
        out_shape=jax.ShapeDtypeStruct((8, 2, CH, CH), jnp.float32),
        scratch_shapes=[pltpu.VMEM((64 * PITCH, 128), jnp.float32)],
        compiler_params=pltpu.CompilerParams(vmem_limit_bytes=24 * MIB),
        name="cross",
    )(x.reshape(64 * 64, 128))


def moments_kernel(
    lev_vec, roll_vec, x_ref, lm_hbm, sp_hbm, rm_hbm, sums, rolls, squares, lm, sp, rm, sems
):
    row = lax.broadcasted_iota(jnp.int32, (CH, CH), 0)
    col = lax.broadcasted_iota(jnp.int32, (CH, CH), 1)
    levels, turns = lev_vec[...], roll_vec[...]
    lev_ref = [levels[0, r] for r in range(RUNS)]
    roll_ref = [turns[0, r] for r in range(RUNS)]
    sums[...] = jnp.zeros_like(sums)
    rolls[...] = jnp.zeros_like(rolls)
    squares[...] = jnp.zeros_like(squares)

    def unpack(m):
        t = m.T
        real = jnp.where(row >= col, m, t)
        imag = jnp.where(row < col, m, jnp.where(row > col, -t, 0.0))
        return real, imag

    def count(ref, level):
        total = jnp.int32(0)
        for r in range(RUNS):
            total += (ref[r] == level).astype(jnp.int32)
        return jnp.maximum(total, 1).astype(jnp.float32)

    sends = []

    def send(source, target, kind, level):
        copy = pltpu.make_async_copy(source.at[level], target.at[level], sems.at[kind, level])
        copy.start()
        sends.append(copy)

    for r in range(RUNS):
        rolls[roll_ref[r]] += x_ref[r]
    for q in range(NQ):
        rm[q, 0, 0], rm[q, 0, 1] = unpack(rolls[q] / count(roll_ref, q))
        send(rm, rm_hbm, 0, q)
    for r in range(RUNS):
        sums[lev_ref[r]] += x_ref[r]
    for l in range(NC):
        mean = sums[l] / count(lev_ref, l)
        sums[l] = mean
        lm[l, 0, 0], lm[l, 0, 1] = unpack(mean)
        send(lm, lm_hbm, 1, l)
    for r in range(RUNS):
        level = lev_ref[r]
        offset = x_ref[r] - sums[level]
        squares[level] += offset * offset
    for l in range(NC):
        s = squares[l]
        sp[l, 0] = BIN * jnp.where(row == col, s, s + s.T)
        send(sp, sp_hbm, 2, l)
    for copy in sends:
        copy.wait()


def moments(cohesion, rolling, x):
    vmem = pl.BlockSpec(memory_space=pltpu.VMEM)
    smem = pl.BlockSpec(memory_space=pltpu.SMEM)
    hbm = pl.BlockSpec(memory_space=pltpu.HBM)
    shapes = [(NC, 1, 2, CH, CH), (NC, 1, CH, CH), (NQ, 1, 2, CH, CH)]
    return pl.pallas_call(
        moments_kernel,
        in_specs=[vmem, vmem, vmem],
        out_specs=(hbm, hbm, hbm),
        out_shape=tuple(jax.ShapeDtypeStruct(shape, jnp.float32) for shape in shapes),
        scratch_shapes=[pltpu.VMEM((4, CH, CH), jnp.float32)] * 3
        + [pltpu.VMEM(shape, jnp.float32) for shape in shapes]
        + [pltpu.SemaphoreType.DMA((3, 4))],
        compiler_params=pltpu.CompilerParams(vmem_limit_bytes=16 * MIB),
        name="moments",
    )(cohesion.reshape(1, RUNS), rolling.reshape(1, RUNS), x.reshape(RUNS, CH, CH))


def exchange(x, axis):
    return lax.all_to_all(x, axis, split_axis=0, concat_axis=0, tiled=True)


def per_device(samples, cohesion, rolling):
    series = exchange(pack(samples).reshape(64, 64, 128), "tm")
    bins = dft(series.reshape(64, 2, 2, 2, 8, 128))
    band = exchange(bins.reshape(64, 64, 128), "tm")
    gathered = exchange(cross(band), "runs")
    return moments(cohesion, rolling, gathered)


def solution(mesh):
    return jax.shard_map(
        per_device,
        mesh=mesh,
        in_specs=(P("runs", "tm", None), P(), P()),
        out_specs=(
            P(None, "tm", None, None, None),
            P(None, "tm", None, None),
            P(None, "tm", None, None, None),
        ),
        check_vma=False,
    )
```

```python
import functools
import math

import jax
import jax.numpy as jnp
import ml_dtypes
import numpy as np
from jax import lax
from jax.experimental import pallas as pl
from jax.experimental.pallas import tpu as pltpu
from jax.sharding import PartitionSpec as P

CH = 128
BIN = 1024
NC = 4
NQ = 4
TOTAL = 131072
RUNS = 16
NB = 64
T1 = 512
T2 = 256

NT = (((1,), (1,)), ((), ()))
MIB = 1 << 20
PITCH = 72
STEP = 136


def split_table(table):
    high = table.astype(ml_dtypes.bfloat16)
    low = (table - high.astype(np.float64)).astype(ml_dtypes.bfloat16)
    return high, low


@functools.lru_cache(maxsize=None)
def tables():
    even, odd = np.arange(0, 256, 2), np.arange(1, 256, 2)
    t1 = np.arange(256)

    def trig(k, t, period):
        angle = 2.0 * np.pi * (k[:, None] * t[None, :] % period) / period
        return np.cos(angle), np.sin(angle)

    cos_e, sin_e = trig(even, t1, T1)
    cos_o, sin_o = trig(odd, t1, T1)
    sin_e[0] = -np.cos(np.pi * (t1 % 2))
    first_even = np.concatenate([cos_e, -sin_e], axis=0)
    first_odd = np.concatenate([cos_o, -sin_o], axis=0)
    t2 = np.arange(T2)
    cos_t, sin_t = trig(np.concatenate([even, odd]), t2, TOTAL)
    near = np.arange(128)
    second = np.zeros((2, NB, 2, 2, 2, 128))
    edge = np.zeros((NB, 8, T2))
    for band in range(NB):
        for parity in range(2):
            for m, (k2, sign) in enumerate(
                [(2 * band + parity, 1.0), (254 + parity - 2 * band, -1.0)]
            ):
                a = 2.0 * np.pi * (k2 * near % T2) / T2
                second[parity, band, 0, m, 0] = np.cos(a)
                second[parity, band, 0, m, 1] = np.sin(a)
                second[parity, band, 1, m, 0] = -sign * np.sin(a)
                second[parity, band, 1, m, 1] = sign * np.cos(a)
        for half in range(2):
            for m in range(2):
                a = 2.0 * np.pi * ((2 * (2 * band + m) + half) * t2 % 512) / 512
                edge[band, 4 * half + m] = np.cos(a)
                edge[band, 4 * half + 2 + m] = -np.sin(a)
    t = np.arange(TOTAL).reshape(T1, T2)
    window = 0.5 - 0.5 * np.cos(2.0 * np.pi * t / TOTAL)

    def passes(table):
        high, low = split_table(table)
        return np.concatenate([high, high, low], axis=1)

    return (
        window.astype(np.float32),
        cos_t.astype(np.float32),
        sin_t.astype(np.float32),
        passes(first_even),
        passes(first_odd),
        passes(second[0].reshape(256, 256)),
        passes(second[1].reshape(256, 256)),
        passes(edge.reshape(NB * 8, T2)),
    )


def split(value):
    high = value.astype(jnp.bfloat16)
    low = (value - high.astype(jnp.float32)).astype(jnp.bfloat16)
    return high, low


def dot(a, b):
    return jnp.dot(a, b, preferred_element_type=jnp.float32)


def dot_nt(a, b):
    return lax.dot_general(a, b, NT, preferred_element_type=jnp.float32)


def pack_kernel(x_hbm, o_ref, landed, turned, sems):
    copies = [
        pltpu.make_async_copy(x_hbm.at[r, :, h], landed.at[r, h], sems.at[r, h])
        for r in range(2)
        for h in range(2)
    ]
    for copy in copies:
        copy.start()
    for r in range(2):
        for h in range(2):
            copies[2 * r + h].wait()
            for u in range(8):
                turned[r, h, u * STEP : u * STEP + 128, :] = landed[r, h, u].T
            for ch in range(CH):
                o_ref[ch % 64, ch // 64, r, h] = turned[r, h, pl.ds(ch, 8, stride=STEP), :]


def pack(samples):
    x = samples.reshape(2, 8, 2, 128, CH)
    return pl.pallas_call(
        pack_kernel,
        in_specs=[pl.BlockSpec(memory_space=pltpu.HBM)],
        out_specs=pl.BlockSpec(memory_space=pltpu.VMEM),
        out_shape=jax.ShapeDtypeStruct((64, 2, 2, 2, 8, 128), jnp.float32),
        scratch_shapes=[
            pltpu.VMEM((2, 2, 8, 128, CH), jnp.float32),
            pltpu.VMEM((2, 2, 9 * STEP, 128), jnp.float32),
            pltpu.SemaphoreType.DMA((2, 2)),
        ],
        compiler_params=pltpu.CompilerParams(vmem_limit_bytes=50 * MIB),
        name="pack",
    )(x)


def dft_kernel(
    x_ref, w_ref, c_ref, s_ref, fe_ref, fo_ref, se_ref, so_ref, edge_ref, o_ref, edge_in, middle
):
    edge_in[...] = jnp.zeros_like(edge_in)
    first_row = lax.broadcasted_iota(jnp.int32, (256, T2), 0) == 0
    upper = lax.broadcasted_iota(jnp.int32, (32, 8, 128), 1) < 4

    for i in range(4):
        halves = [x_ref[:, i // 2, i % 2, h].reshape(T1, 128) for h in range(2)]
        x = jnp.concatenate(halves, axis=1) * w_ref[...]
        xh, xl = split(x[:256] + x[256:])
        a_even = dot(fe_ref[...], jnp.concatenate([xh, xl, xh], axis=0))
        xh, xl = split(x[:256] - x[256:])
        a_odd = dot(fo_ref[...], jnp.concatenate([xh, xl, xh], axis=0))
        a_re = jnp.concatenate([a_even[:128], a_odd[:128]], axis=0)
        a_im = jnp.concatenate([a_even[128:], a_odd[128:]], axis=0)
        c, s = c_ref[...], s_ref[...]
        b_re = a_re * c + a_im * s
        b_im = a_im * c - a_re * s
        edge_in[i : i + 1, :] = b_re[:1]
        edge_in[i + 4 : i + 5, :] = b_im[:1]
        b_re = jnp.where(first_row, 0.0, b_re)
        b_im = jnp.where(first_row, 0.0, b_im)
        plus = jnp.concatenate(
            [b_re[:, :128] + b_re[:, 128:], b_im[:, :128] + b_im[:, 128:]], axis=1
        )
        minus = jnp.concatenate(
            [b_re[:, :128] - b_re[:, 128:], b_im[:, :128] - b_im[:, 128:]], axis=1
        )
        middle[i, 0, 0], middle[i, 0, 1] = split(plus)
        middle[i, 1, 0], middle[i, 1, 1] = split(minus)

    eh, el = split(edge_in[...])
    edge = dot_nt(edge_ref[...], jnp.concatenate([eh, el, eh], axis=1))
    first_lane = lax.broadcasted_iota(jnp.int32, (512, 128), 1) == 0
    sub = lax.broadcasted_iota(jnp.int32, (512, 128), 0) % 8 < 4

    for i in range(4):
        bh, bl = middle[i, 0, 0], middle[i, 0, 1]
        o_even = dot_nt(se_ref[...], jnp.concatenate([bh, bl, bh], axis=1))
        bh, bl = middle[i, 1, 0], middle[i, 1, 1]
        o_odd = dot_nt(so_ref[...], jnp.concatenate([bh, bl, bh], axis=1))
        low = edge if i == 0 else pltpu.roll(edge, 128 - i, 1)
        extra = jnp.where(sub, low, pltpu.roll(edge, 124 - i, 1))
        extra = jnp.where(first_lane, extra, 0.0).reshape(32, 2, 8, 128)
        for half in range(2):
            lanes = slice(128 * half, 128 * half + 128)
            e = o_even[:, lanes].reshape(32, 8, 128)
            o = o_odd[:, lanes].reshape(32, 8, 128)
            first = jnp.where(upper, e, pltpu.roll(o, 4, 1))
            second = jnp.where(upper, pltpu.roll(e, 4, 1), o)
            o_ref[:, 0, i, half] = first + extra[:, 0] if half == 0 else first
            o_ref[:, 1, i, half] = second + extra[:, 1] if half == 0 else second


def dft(x):
    consts = [jnp.asarray(t) for t in tables()]
    vmem = pl.BlockSpec(memory_space=pltpu.VMEM)
    return pl.pallas_call(
        dft_kernel,
        in_specs=[vmem] * (1 + len(consts)),
        out_specs=vmem,
        out_shape=jax.ShapeDtypeStruct((NB // 2, 2, 4, 2, 8, 128), jnp.float32),
        scratch_shapes=[
            pltpu.VMEM((128, T2), jnp.float32),
            pltpu.VMEM((4, 2, 2, 256, 256), jnp.bfloat16),
        ],
        compiler_params=pltpu.CompilerParams(vmem_limit_bytes=24 * MIB),
        name="dft",
    )(x, *consts)


def cross_kernel(x_ref, o_ref, rows, *, scale):
    row = lax.broadcasted_iota(jnp.int32, (CH, CH), 0)
    col = lax.broadcasted_iota(jnp.int32, (CH, CH), 1)
    for q in range(64):
        rows[q * PITCH : q * PITCH + 64, :] = x_ref[q * 64 : q * 64 + 64, :]
    for r in range(2):
        parts = []
        for part in range(2):
            for c in range(2):
                cols = [
                    rows[pl.ds((c * 2 + r) * 16 + half * 8 + part * 2 + m, 64, stride=PITCH), :]
                    for m in (0, 1, 4, 5)
                    for half in range(2)
                ]
                parts.append(jnp.concatenate(cols, axis=1))
        v = jnp.concatenate(parts, axis=0)
        vh, vl = split(v)
        mixed = dot_nt(vh, vl)
        g = dot_nt(vh, vh) + (mixed + mixed.T)
        real = g[:CH, :CH] + g[CH:, CH:]
        imag = g[CH:, :CH] - g[:CH, CH:]
        packed = jnp.where(row >= col, real, imag) * scale
        for y in range(8):
            o_ref[y, r] = packed


def cross(x):
    scale = 1.0 / (0.375 * BIN * TOTAL)
    return pl.pallas_call(
        functools.partial(cross_kernel, scale=scale),
        in_specs=[pl.BlockSpec(memory_space=pltpu.VMEM)],
        out_specs=pl.BlockSpec(memory_space=pltpu.VMEM),
        out_shape=jax.ShapeDtypeStruct((8, 2, CH, CH), jnp.float32),
        scratch_shapes=[pltpu.VMEM((65 * PITCH, 128), jnp.float32)],
        compiler_params=pltpu.CompilerParams(vmem_limit_bytes=24 * MIB),
        name="cross",
    )(x.reshape(64 * 64, 128))


def moments_kernel(
    lev_vec, roll_vec, x_ref, lm_hbm, sp_hbm, rm_hbm, sums, rolls, squares, lm, sp, rm, sems
):
    row = lax.broadcasted_iota(jnp.int32, (CH, CH), 0)
    col = lax.broadcasted_iota(jnp.int32, (CH, CH), 1)
    levels, turns = lev_vec[...], roll_vec[...]
    lev_ref = [levels[0, r] for r in range(RUNS)]
    roll_ref = [turns[0, r] for r in range(RUNS)]
    sums[...] = jnp.zeros_like(sums)
    rolls[...] = jnp.zeros_like(rolls)
    squares[...] = jnp.zeros_like(squares)

    def unpack(m):
        t = m.T
        real = jnp.where(row >= col, m, t)
        imag = jnp.where(row < col, m, jnp.where(row > col, -t, 0.0))
        return real, imag

    def count(ref, level):
        total = jnp.int32(0)
        for r in range(RUNS):
            total += (ref[r] == level).astype(jnp.int32)
        return jnp.maximum(total, 1).astype(jnp.float32)

    sends = []

    def send(source, target, kind, level):
        copy = pltpu.make_async_copy(source.at[level], target.at[level], sems.at[kind, level])
        copy.start()
        sends.append(copy)

    for r in range(RUNS):
        rolls[roll_ref[r]] += x_ref[r]
    for q in range(NQ):
        rm[q, 0, 0], rm[q, 0, 1] = unpack(rolls[q] / count(roll_ref, q))
        send(rm, rm_hbm, 0, q)
    for r in range(RUNS):
        sums[lev_ref[r]] += x_ref[r]
    for l in range(NC):
        mean = sums[l] / count(lev_ref, l)
        sums[l] = mean
        lm[l, 0, 0], lm[l, 0, 1] = unpack(mean)
        send(lm, lm_hbm, 1, l)
    for r in range(RUNS):
        level = lev_ref[r]
        offset = x_ref[r] - sums[level]
        squares[level] += offset * offset
    for l in range(NC):
        s = squares[l]
        sp[l, 0] = BIN * jnp.where(row == col, s, s + s.T)
        send(sp, sp_hbm, 2, l)
    for copy in sends:
        copy.wait()


def moments(cohesion, rolling, x):
    vmem = pl.BlockSpec(memory_space=pltpu.VMEM)
    smem = pl.BlockSpec(memory_space=pltpu.SMEM)
    hbm = pl.BlockSpec(memory_space=pltpu.HBM)
    shapes = [(NC, 1, 2, CH, CH), (NC, 1, CH, CH), (NQ, 1, 2, CH, CH)]
    return pl.pallas_call(
        moments_kernel,
        in_specs=[vmem, vmem, vmem],
        out_specs=(hbm, hbm, hbm),
        out_shape=tuple(jax.ShapeDtypeStruct(shape, jnp.float32) for shape in shapes),
        scratch_shapes=[pltpu.VMEM((4, CH, CH), jnp.float32)] * 3
        + [pltpu.VMEM(shape, jnp.float32) for shape in shapes]
        + [pltpu.SemaphoreType.DMA((3, 4))],
        compiler_params=pltpu.CompilerParams(vmem_limit_bytes=16 * MIB),
        name="moments",
    )(cohesion.reshape(1, RUNS), rolling.reshape(1, RUNS), x.reshape(RUNS, CH, CH))


def exchange(x, axis):
    return lax.all_to_all(x, axis, split_axis=0, concat_axis=0, tiled=True)


def per_device(samples, cohesion, rolling):
    series = exchange(pack(samples).reshape(64, 64, 128), "tm")
    bins = dft(series.reshape(64, 2, 2, 2, 8, 128))
    band = exchange(bins.reshape(64, 64, 128), "tm")
    gathered = exchange(cross(band), "runs")
    return moments(cohesion, rolling, gathered)


def solution(mesh):
    return jax.shard_map(
        per_device,
        mesh=mesh,
        in_specs=(P("runs", "tm", None), P(), P()),
        out_specs=(
            P(None, "tm", None, None, None),
            P(None, "tm", None, None),
            P(None, "tm", None, None, None),
        ),
        check_vma=False,
    )
```

```python
import functools
import math

import jax
import jax.numpy as jnp
import ml_dtypes
import numpy as np
from jax import lax
from jax.experimental import pallas as pl
from jax.experimental.pallas import tpu as pltpu
from jax.sharding import PartitionSpec as P

CH = 128
BIN = 1024
NC = 4
NQ = 4
TOTAL = 131072
RUNS = 16
NB = 64
T1 = 512
T2 = 256

NT = (((1,), (1,)), ((), ()))
MIB = 1 << 20
PITCH = 136
STEP = 136


def split_table(table):
    high = table.astype(ml_dtypes.bfloat16)
    low = (table - high.astype(np.float64)).astype(ml_dtypes.bfloat16)
    return high, low


@functools.lru_cache(maxsize=None)
def tables():
    even, odd = np.arange(0, 256, 2), np.arange(1, 256, 2)
    t1 = np.arange(256)

    def trig(k, t, period):
        angle = 2.0 * np.pi * (k[:, None] * t[None, :] % period) / period
        return np.cos(angle), np.sin(angle)

    cos_e, sin_e = trig(even, t1, T1)
    cos_o, sin_o = trig(odd, t1, T1)
    sin_e[0] = -np.cos(np.pi * (t1 % 2))
    first_even = np.concatenate([cos_e, -sin_e], axis=0)
    first_odd = np.concatenate([cos_o, -sin_o], axis=0)
    t2 = np.arange(T2)
    cos_t, sin_t = trig(np.concatenate([even, odd]), t2, TOTAL)
    near = np.arange(128)
    second = np.zeros((2, NB, 2, 2, 2, 128))
    edge = np.zeros((NB, 8, T2))
    for band in range(NB):
        for parity in range(2):
            for m, (k2, sign) in enumerate(
                [(2 * band + parity, 1.0), (254 + parity - 2 * band, -1.0)]
            ):
                a = 2.0 * np.pi * (k2 * near % T2) / T2
                second[parity, band, 0, m, 0] = np.cos(a)
                second[parity, band, 0, m, 1] = np.sin(a)
                second[parity, band, 1, m, 0] = -sign * np.sin(a)
                second[parity, band, 1, m, 1] = sign * np.cos(a)
        for half in range(2):
            for m in range(2):
                a = 2.0 * np.pi * ((2 * (2 * band + m) + half) * t2 % 512) / 512
                edge[band, 4 * half + m] = np.cos(a)
                edge[band, 4 * half + 2 + m] = -np.sin(a)
    t = np.arange(TOTAL).reshape(T1, T2)
    window = 0.5 - 0.5 * np.cos(2.0 * np.pi * t / TOTAL)

    def passes(table):
        high, low = split_table(table)
        return np.concatenate([high, high, low], axis=1)

    return (
        window.astype(np.float32),
        cos_t.astype(np.float32),
        sin_t.astype(np.float32),
        passes(first_even),
        passes(first_odd),
        passes(second[0].reshape(256, 256)),
        passes(second[1].reshape(256, 256)),
        passes(edge.reshape(NB * 8, T2)),
    )


def split(value):
    high = value.astype(jnp.bfloat16)
    low = (value - high.astype(jnp.float32)).astype(jnp.bfloat16)
    return high, low


def dot(a, b):
    return jnp.dot(a, b, preferred_element_type=jnp.float32)


def dot_nt(a, b):
    return lax.dot_general(a, b, NT, preferred_element_type=jnp.float32)


def pack_kernel(x_hbm, o_ref, landed, turned, sems):
    copies = [
        pltpu.make_async_copy(x_hbm.at[r, :, h], landed.at[r, h], sems.at[r, h])
        for r in range(2)
        for h in range(2)
    ]
    for copy in copies:
        copy.start()
    for r in range(2):
        for h in range(2):
            copies[2 * r + h].wait()
            for u in range(8):
                turned[r, h, u * STEP : u * STEP + 128, :] = landed[r, h, u].T
            for ch in range(CH):
                o_ref[ch % 32, r, ch // 32, h] = turned[r, h, pl.ds(ch, 8, stride=STEP), :]


def pack(samples):
    x = samples.reshape(2, 8, 2, 128, CH)
    return pl.pallas_call(
        pack_kernel,
        in_specs=[pl.BlockSpec(memory_space=pltpu.HBM)],
        out_specs=pl.BlockSpec(memory_space=pltpu.VMEM),
        out_shape=jax.ShapeDtypeStruct((32, 2, 4, 2, 8, 128), jnp.float32),
        scratch_shapes=[
            pltpu.VMEM((2, 2, 8, 128, CH), jnp.float32),
            pltpu.VMEM((2, 2, 9 * STEP, 128), jnp.float32),
            pltpu.SemaphoreType.DMA((2, 2)),
        ],
        compiler_params=pltpu.CompilerParams(vmem_limit_bytes=50 * MIB),
        name="pack",
    )(x)


def dft_kernel(
    x_ref, w_ref, c_ref, s_ref, fe_ref, fo_ref, se_ref, so_ref, edge_ref, o_ref, edge_in, middle
):
    edge_in[...] = jnp.zeros_like(edge_in)
    first_row = lax.broadcasted_iota(jnp.int32, (256, T2), 0) == 0
    upper = lax.broadcasted_iota(jnp.int32, (32, 8, 128), 1) < 4

    for i in range(4):
        halves = [x_ref[:, i, h].reshape(T1, 128) for h in range(2)]
        x = jnp.concatenate(halves, axis=1) * w_ref[...]
        xh, xl = split(x[:256] + x[256:])
        a_even = dot(fe_ref[...], jnp.concatenate([xh, xl, xh], axis=0))
        xh, xl = split(x[:256] - x[256:])
        a_odd = dot(fo_ref[...], jnp.concatenate([xh, xl, xh], axis=0))
        a_re = jnp.concatenate([a_even[:128], a_odd[:128]], axis=0)
        a_im = jnp.concatenate([a_even[128:], a_odd[128:]], axis=0)
        c, s = c_ref[...], s_ref[...]
        b_re = a_re * c + a_im * s
        b_im = a_im * c - a_re * s
        edge_in[i : i + 1, :] = b_re[:1]
        edge_in[i + 4 : i + 5, :] = b_im[:1]
        b_re = jnp.where(first_row, 0.0, b_re)
        b_im = jnp.where(first_row, 0.0, b_im)
        plus = jnp.concatenate(
            [b_re[:, :128] + b_re[:, 128:], b_im[:, :128] + b_im[:, 128:]], axis=1
        )
        minus = jnp.concatenate(
            [b_re[:, :128] - b_re[:, 128:], b_im[:, :128] - b_im[:, 128:]], axis=1
        )
        middle[i, 0, 0], middle[i, 0, 1] = split(plus)
        middle[i, 1, 0], middle[i, 1, 1] = split(minus)

    eh, el = split(edge_in[...])
    edge = dot_nt(edge_ref[...], jnp.concatenate([eh, el, eh], axis=1))
    first_lane = lax.broadcasted_iota(jnp.int32, (512, 128), 1) == 0
    sub = lax.broadcasted_iota(jnp.int32, (512, 128), 0) % 8 < 4

    for i in range(4):
        bh, bl = middle[i, 0, 0], middle[i, 0, 1]
        o_even = dot_nt(se_ref[...], jnp.concatenate([bh, bl, bh], axis=1))
        bh, bl = middle[i, 1, 0], middle[i, 1, 1]
        o_odd = dot_nt(so_ref[...], jnp.concatenate([bh, bl, bh], axis=1))
        low = edge if i == 0 else pltpu.roll(edge, 128 - i, 1)
        extra = jnp.where(sub, low, pltpu.roll(edge, 124 - i, 1))
        extra = jnp.where(first_lane, extra, 0.0).reshape(32, 2, 8, 128)
        for half in range(2):
            lanes = slice(128 * half, 128 * half + 128)
            e = o_even[:, lanes].reshape(32, 8, 128)
            o = o_odd[:, lanes].reshape(32, 8, 128)
            first = jnp.where(upper, e, pltpu.roll(o, 4, 1))
            second = jnp.where(upper, pltpu.roll(e, 4, 1), o)
            o_ref[:, 0, i, half] = first + extra[:, 0] if half == 0 else first
            o_ref[:, 1, i, half] = second + extra[:, 1] if half == 0 else second


def dft(x):
    consts = [jnp.asarray(t) for t in tables()]
    vmem = pl.BlockSpec(memory_space=pltpu.VMEM)
    return pl.pallas_call(
        dft_kernel,
        in_specs=[vmem] * (1 + len(consts)),
        out_specs=vmem,
        out_shape=jax.ShapeDtypeStruct((NB // 2, 2, 4, 2, 8, 128), jnp.float32),
        scratch_shapes=[
            pltpu.VMEM((128, T2), jnp.float32),
            pltpu.VMEM((4, 2, 2, 256, 256), jnp.bfloat16),
        ],
        compiler_params=pltpu.CompilerParams(vmem_limit_bytes=24 * MIB),
        name="dft",
    )(x, *consts)


def cross_kernel(x_ref, o_ref, rows, *, scale):
    row = lax.broadcasted_iota(jnp.int32, (CH, CH), 0)
    col = lax.broadcasted_iota(jnp.int32, (CH, CH), 1)
    for chip in range(32):
        rows[chip * PITCH : chip * PITCH + 128, :] = x_ref[chip * 128 : chip * 128 + 128, :]
    for band in range(2):
        parts = []
        for part in range(2):
            for c in range(4):
                cols = [
                    rows[pl.ds((band * 4 + c) * 16 + half * 8 + part * 2 + m, 32, stride=PITCH), :]
                    for m in (0, 1, 4, 5)
                    for half in range(2)
                ]
                parts.append(jnp.concatenate(cols, axis=1))
        v = jnp.concatenate(parts, axis=0)
        vh, vl = split(v)
        mixed = dot_nt(vh, vl)
        g = dot_nt(vh, vh) + (mixed + mixed.T)
        real = g[:CH, :CH] + g[CH:, CH:]
        imag = g[CH:, :CH] - g[:CH, CH:]
        packed = jnp.where(row >= col, real, imag) * scale
        for y in range(8):
            o_ref[band * 8 + y] = packed


def cross(x):
    scale = 1.0 / (0.375 * BIN * TOTAL)
    return pl.pallas_call(
        functools.partial(cross_kernel, scale=scale),
        in_specs=[pl.BlockSpec(memory_space=pltpu.VMEM)],
        out_specs=pl.BlockSpec(memory_space=pltpu.VMEM),
        out_shape=jax.ShapeDtypeStruct((16, CH, CH), jnp.float32),
        scratch_shapes=[pltpu.VMEM((33 * PITCH, 128), jnp.float32)],
        compiler_params=pltpu.CompilerParams(vmem_limit_bytes=24 * MIB),
        name="cross",
    )(x.reshape(64 * 64, 128))


def moments_kernel(
    lev_vec, roll_vec, x_ref, lm_hbm, sp_hbm, rm_hbm, sums, rolls, squares, lm, sp, rm, sems
):
    row = lax.broadcasted_iota(jnp.int32, (CH, CH), 0)
    col = lax.broadcasted_iota(jnp.int32, (CH, CH), 1)
    levels, turns = lev_vec[...], roll_vec[...]
    order = [2 * (k % 8) + k // 8 for k in range(RUNS)]
    lev_ref = [levels[0, r] for r in order]
    roll_ref = [turns[0, r] for r in order]
    sums[...] = jnp.zeros_like(sums)
    rolls[...] = jnp.zeros_like(rolls)
    squares[...] = jnp.zeros_like(squares)

    def unpack(m):
        t = m.T
        real = jnp.where(row >= col, m, t)
        imag = jnp.where(row < col, m, jnp.where(row > col, -t, 0.0))
        return real, imag

    def count(ref, level):
        total = jnp.int32(0)
        for r in range(RUNS):
            total += (ref[r] == level).astype(jnp.int32)
        return jnp.maximum(total, 1).astype(jnp.float32)

    sends = []

    def send(source, target, kind, level):
        copy = pltpu.make_async_copy(source.at[level], target.at[level], sems.at[kind, level])
        copy.start()
        sends.append(copy)

    for r in range(RUNS):
        rolls[roll_ref[r]] += x_ref[r]
    for q in range(NQ):
        rm[q, 0, 0], rm[q, 0, 1] = unpack(rolls[q] / count(roll_ref, q))
        send(rm, rm_hbm, 0, q)
    for r in range(RUNS):
        sums[lev_ref[r]] += x_ref[r]
    for l in range(NC):
        mean = sums[l] / count(lev_ref, l)
        sums[l] = mean
        lm[l, 0, 0], lm[l, 0, 1] = unpack(mean)
        send(lm, lm_hbm, 1, l)
    for r in range(RUNS):
        level = lev_ref[r]
        offset = x_ref[r] - sums[level]
        squares[level] += offset * offset
    for l in range(NC):
        s = squares[l]
        sp[l, 0] = BIN * jnp.where(row == col, s, s + s.T)
        send(sp, sp_hbm, 2, l)
    for copy in sends:
        copy.wait()


def moments(cohesion, rolling, x):
    vmem = pl.BlockSpec(memory_space=pltpu.VMEM)
    smem = pl.BlockSpec(memory_space=pltpu.SMEM)
    hbm = pl.BlockSpec(memory_space=pltpu.HBM)
    shapes = [(NC, 1, 2, CH, CH), (NC, 1, CH, CH), (NQ, 1, 2, CH, CH)]
    return pl.pallas_call(
        moments_kernel,
        in_specs=[vmem, vmem, vmem],
        out_specs=(hbm, hbm, hbm),
        out_shape=tuple(jax.ShapeDtypeStruct(shape, jnp.float32) for shape in shapes),
        scratch_shapes=[pltpu.VMEM((4, CH, CH), jnp.float32)] * 3
        + [pltpu.VMEM(shape, jnp.float32) for shape in shapes]
        + [pltpu.SemaphoreType.DMA((3, 4))],
        compiler_params=pltpu.CompilerParams(vmem_limit_bytes=16 * MIB),
        name="moments",
    )(cohesion.reshape(1, RUNS), rolling.reshape(1, RUNS), x)


def exchange(x, axis, groups=None):
    return lax.all_to_all(
        x, axis, split_axis=0, concat_axis=0, tiled=True, axis_index_groups=groups
    )


def per_device(samples, cohesion, rolling):
    same_core = [[2 * chip + core for chip in range(32)] for core in range(2)]
    column = [[16 * chip + k for k in range(16)] for chip in range(32)]
    series = exchange(pack(samples).reshape(64, 64, 128), "tm")
    bins = dft(series.reshape(64, 4, 2, 8, 128))
    bands = exchange(bins.reshape(32, 128, 128), "tm", same_core)
    gathered = exchange(cross(bands), ("tm", "runs"), column)
    return moments(cohesion, rolling, gathered)


def solution(mesh):
    return jax.shard_map(
        per_device,
        mesh=mesh,
        in_specs=(P("runs", "tm", None), P(), P()),
        out_specs=(
            P(None, "tm", None, None, None),
            P(None, "tm", None, None),
            P(None, "tm", None, None, None),
        ),
        check_vma=False,
    )
```

```python
import functools
import math

import jax
import jax.numpy as jnp
import ml_dtypes
import numpy as np
from jax import lax
from jax.experimental import pallas as pl
from jax.experimental.pallas import tpu as pltpu
from jax.sharding import PartitionSpec as P

CH = 128
BIN = 1024
NC = 4
NQ = 4
TOTAL = 131072
RUNS = 16
NB = 64
T1 = 512
T2 = 256

NT = (((1,), (1,)), ((), ()))
MIB = 1 << 20
PITCH = 72
STEP = 136
RING = [0, 5, 2, 7, 4, 1, 6, 3]


def split_table(table):
    high = table.astype(ml_dtypes.bfloat16)
    low = (table - high.astype(np.float64)).astype(ml_dtypes.bfloat16)
    return high, low


@functools.lru_cache(maxsize=None)
def tables():
    even, odd = np.arange(0, 256, 2), np.arange(1, 256, 2)
    t1 = np.arange(256)

    def trig(k, t, period):
        angle = 2.0 * np.pi * (k[:, None] * t[None, :] % period) / period
        return np.cos(angle), np.sin(angle)

    cos_e, sin_e = trig(even, t1, T1)
    cos_o, sin_o = trig(odd, t1, T1)
    sin_e[0] = -np.cos(np.pi * (t1 % 2))
    first_even = np.concatenate([cos_e, -sin_e], axis=0)
    first_odd = np.concatenate([cos_o, -sin_o], axis=0)
    t2 = np.arange(T2)
    cos_t, sin_t = trig(np.concatenate([even, odd]), t2, TOTAL)
    near = np.arange(128)
    second = np.zeros((2, NB, 2, 2, 2, 128))
    edge = np.zeros((NB, 8, T2))
    for band in range(NB):
        for parity in range(2):
            for m, (k2, sign) in enumerate(
                [(2 * band + parity, 1.0), (254 + parity - 2 * band, -1.0)]
            ):
                a = 2.0 * np.pi * (k2 * near % T2) / T2
                second[parity, band, 0, m, 0] = np.cos(a)
                second[parity, band, 0, m, 1] = np.sin(a)
                second[parity, band, 1, m, 0] = -sign * np.sin(a)
                second[parity, band, 1, m, 1] = sign * np.cos(a)
        for half in range(2):
            for m in range(2):
                a = 2.0 * np.pi * ((2 * (2 * band + m) + half) * t2 % 512) / 512
                edge[band, 4 * half + m] = np.cos(a)
                edge[band, 4 * half + 2 + m] = -np.sin(a)
    t = np.arange(TOTAL).reshape(T1, T2)
    window = 0.5 - 0.5 * np.cos(2.0 * np.pi * t / TOTAL)

    def passes(table):
        high, low = split_table(table)
        return np.concatenate([high, high, low], axis=1)

    return (
        window.astype(np.float32),
        cos_t.astype(np.float32),
        sin_t.astype(np.float32),
        passes(first_even),
        passes(first_odd),
        passes(second[0].reshape(256, 256)),
        passes(second[1].reshape(256, 256)),
        passes(edge.reshape(NB * 8, T2)),
    )


def split(value):
    high = value.astype(jnp.bfloat16)
    low = (value - high.astype(jnp.float32)).astype(jnp.bfloat16)
    return high, low


def dot(a, b):
    return jnp.dot(a, b, preferred_element_type=jnp.float32)


def dot_nt(a, b):
    return lax.dot_general(a, b, NT, preferred_element_type=jnp.float32)


def pack_kernel(x_hbm, o_ref, landed, turned, sems):
    copies = [
        pltpu.make_async_copy(x_hbm.at[r, :, h], landed.at[r, h], sems.at[r, h])
        for r in range(2)
        for h in range(2)
    ]
    for copy in copies:
        copy.start()
    for r in range(2):
        for h in range(2):
            copies[2 * r + h].wait()
            for u in range(8):
                turned[r, h, u * STEP : u * STEP + 128, :] = landed[r, h, u].T
            for ch in range(CH):
                o_ref[ch % 64, ch // 64, r, h] = turned[r, h, pl.ds(ch, 8, stride=STEP), :]


def pack(samples):
    x = samples.reshape(2, 8, 2, 128, CH)
    return pl.pallas_call(
        pack_kernel,
        in_specs=[pl.BlockSpec(memory_space=pltpu.HBM)],
        out_specs=pl.BlockSpec(memory_space=pltpu.VMEM),
        out_shape=jax.ShapeDtypeStruct((64, 2, 2, 2, 8, 128), jnp.float32),
        scratch_shapes=[
            pltpu.VMEM((2, 2, 8, 128, CH), jnp.float32),
            pltpu.VMEM((2, 2, 9 * STEP, 128), jnp.float32),
            pltpu.SemaphoreType.DMA((2, 2)),
        ],
        compiler_params=pltpu.CompilerParams(vmem_limit_bytes=50 * MIB),
        name="pack",
    )(x)


def dft_kernel(
    x_ref, w_ref, c_ref, s_ref, fe_ref, fo_ref, se_ref, so_ref, edge_ref, o_ref, edge_in, middle
):
    edge_in[...] = jnp.zeros_like(edge_in)
    first_row = lax.broadcasted_iota(jnp.int32, (256, T2), 0) == 0
    upper = lax.broadcasted_iota(jnp.int32, (32, 8, 128), 1) < 4

    for i in range(4):
        halves = [x_ref[:, i // 2, i % 2, h].reshape(T1, 128) for h in range(2)]
        x = jnp.concatenate(halves, axis=1) * w_ref[...]
        xh, xl = split(x[:256] + x[256:])
        a_even = dot(fe_ref[...], jnp.concatenate([xh, xl, xh], axis=0))
        xh, xl = split(x[:256] - x[256:])
        a_odd = dot(fo_ref[...], jnp.concatenate([xh, xl, xh], axis=0))
        a_re = jnp.concatenate([a_even[:128], a_odd[:128]], axis=0)
        a_im = jnp.concatenate([a_even[128:], a_odd[128:]], axis=0)
        c, s = c_ref[...], s_ref[...]
        b_re = a_re * c + a_im * s
        b_im = a_im * c - a_re * s
        edge_in[i : i + 1, :] = b_re[:1]
        edge_in[i + 4 : i + 5, :] = b_im[:1]
        b_re = jnp.where(first_row, 0.0, b_re)
        b_im = jnp.where(first_row, 0.0, b_im)
        plus = jnp.concatenate(
            [b_re[:, :128] + b_re[:, 128:], b_im[:, :128] + b_im[:, 128:]], axis=1
        )
        minus = jnp.concatenate(
            [b_re[:, :128] - b_re[:, 128:], b_im[:, :128] - b_im[:, 128:]], axis=1
        )
        middle[i, 0, 0], middle[i, 0, 1] = split(plus)
        middle[i, 1, 0], middle[i, 1, 1] = split(minus)

    eh, el = split(edge_in[...])
    edge = dot_nt(edge_ref[...], jnp.concatenate([eh, el, eh], axis=1))
    first_lane = lax.broadcasted_iota(jnp.int32, (512, 128), 1) == 0
    sub = lax.broadcasted_iota(jnp.int32, (512, 128), 0) % 8 < 4

    for i in range(4):
        bh, bl = middle[i, 0, 0], middle[i, 0, 1]
        o_even = dot_nt(se_ref[...], jnp.concatenate([bh, bl, bh], axis=1))
        bh, bl = middle[i, 1, 0], middle[i, 1, 1]
        o_odd = dot_nt(so_ref[...], jnp.concatenate([bh, bl, bh], axis=1))
        low = edge if i == 0 else pltpu.roll(edge, 128 - i, 1)
        extra = jnp.where(sub, low, pltpu.roll(edge, 124 - i, 1))
        extra = jnp.where(first_lane, extra, 0.0).reshape(32, 2, 8, 128)
        for half in range(2):
            lanes = slice(128 * half, 128 * half + 128)
            e = o_even[:, lanes].reshape(32, 8, 128)
            o = o_odd[:, lanes].reshape(32, 8, 128)
            first = jnp.where(upper, e, pltpu.roll(o, 4, 1))
            second = jnp.where(upper, pltpu.roll(e, 4, 1), o)
            o_ref[:, 0, i, half] = first + extra[:, 0] if half == 0 else first
            o_ref[:, 1, i, half] = second + extra[:, 1] if half == 0 else second


def dft(x):
    consts = [jnp.asarray(t) for t in tables()]
    vmem = pl.BlockSpec(memory_space=pltpu.VMEM)
    return pl.pallas_call(
        dft_kernel,
        in_specs=[vmem] * (1 + len(consts)),
        out_specs=vmem,
        out_shape=jax.ShapeDtypeStruct((NB // 2, 2, 4, 2, 8, 128), jnp.float32),
        scratch_shapes=[
            pltpu.VMEM((128, T2), jnp.float32),
            pltpu.VMEM((4, 2, 2, 256, 256), jnp.bfloat16),
        ],
        compiler_params=pltpu.CompilerParams(vmem_limit_bytes=24 * MIB),
        name="dft",
    )(x, *consts)


def cross_kernel(x_ref, o_ref, rows, *, scale):
    row = lax.broadcasted_iota(jnp.int32, (CH, CH), 0)
    col = lax.broadcasted_iota(jnp.int32, (CH, CH), 1)
    for q in range(64):
        rows[q * PITCH : q * PITCH + 64, :] = x_ref[q * 64 : q * 64 + 64, :]
    for r in range(2):
        parts = []
        for part in range(2):
            for c in range(2):
                cols = [
                    rows[pl.ds((c * 2 + r) * 16 + half * 8 + part * 2 + m, 64, stride=PITCH), :]
                    for m in (0, 1, 4, 5)
                    for half in range(2)
                ]
                parts.append(jnp.concatenate(cols, axis=1))
        v = jnp.concatenate(parts, axis=0)
        vh, vl = split(v)
        mixed = dot_nt(vh, vl)
        g = dot_nt(vh, vh) + (mixed + mixed.T)
        real = g[:CH, :CH] + g[CH:, CH:]
        imag = g[CH:, :CH] - g[:CH, CH:]
        packed = jnp.where(row >= col, real, imag) * scale
        for y in range(8):
            o_ref[y, r] = packed


def cross(x):
    scale = 1.0 / (0.375 * BIN * TOTAL)
    return pl.pallas_call(
        functools.partial(cross_kernel, scale=scale),
        in_specs=[pl.BlockSpec(memory_space=pltpu.VMEM)],
        out_specs=pl.BlockSpec(memory_space=pltpu.VMEM),
        out_shape=jax.ShapeDtypeStruct((8, 2, CH, CH), jnp.float32),
        scratch_shapes=[pltpu.VMEM((65 * PITCH, 128), jnp.float32)],
        compiler_params=pltpu.CompilerParams(vmem_limit_bytes=24 * MIB),
        name="cross",
    )(x.reshape(64 * 64, 128))


def moments_kernel(
    lev_vec, roll_vec, x_ref, lm_hbm, sp_hbm, rm_hbm, sums, rolls, squares, lm, sp, rm, sems
):
    row = lax.broadcasted_iota(jnp.int32, (CH, CH), 0)
    col = lax.broadcasted_iota(jnp.int32, (CH, CH), 1)
    levels, turns = lev_vec[...], roll_vec[...]
    order = [2 * y + r for y in RING for r in range(2)]
    lev_ref = [levels[0, r] for r in order]
    roll_ref = [turns[0, r] for r in order]
    sums[...] = jnp.zeros_like(sums)
    rolls[...] = jnp.zeros_like(rolls)
    squares[...] = jnp.zeros_like(squares)

    def unpack(m):
        t = m.T
        real = jnp.where(row >= col, m, t)
        imag = jnp.where(row < col, m, jnp.where(row > col, -t, 0.0))
        return real, imag

    def count(ref, level):
        total = jnp.int32(0)
        for r in range(RUNS):
            total += (ref[r] == level).astype(jnp.int32)
        return jnp.maximum(total, 1).astype(jnp.float32)

    sends = []

    def send(source, target, kind, level):
        copy = pltpu.make_async_copy(source.at[level], target.at[level], sems.at[kind, level])
        copy.start()
        sends.append(copy)

    for r in range(RUNS):
        rolls[roll_ref[r]] += x_ref[r]
    for q in range(NQ):
        rm[q, 0, 0], rm[q, 0, 1] = unpack(rolls[q] / count(roll_ref, q))
        send(rm, rm_hbm, 0, q)
    for r in range(RUNS):
        sums[lev_ref[r]] += x_ref[r]
    for l in range(NC):
        mean = sums[l] / count(lev_ref, l)
        sums[l] = mean
        lm[l, 0, 0], lm[l, 0, 1] = unpack(mean)
        send(lm, lm_hbm, 1, l)
    for r in range(RUNS):
        level = lev_ref[r]
        offset = x_ref[r] - sums[level]
        squares[level] += offset * offset
    for l in range(NC):
        s = squares[l]
        sp[l, 0] = BIN * jnp.where(row == col, s, s + s.T)
        send(sp, sp_hbm, 2, l)
    for copy in sends:
        copy.wait()


def moments(cohesion, rolling, x):
    vmem = pl.BlockSpec(memory_space=pltpu.VMEM)
    smem = pl.BlockSpec(memory_space=pltpu.SMEM)
    hbm = pl.BlockSpec(memory_space=pltpu.HBM)
    shapes = [(NC, 1, 2, CH, CH), (NC, 1, CH, CH), (NQ, 1, 2, CH, CH)]
    return pl.pallas_call(
        moments_kernel,
        in_specs=[vmem, vmem, vmem],
        out_specs=(hbm, hbm, hbm),
        out_shape=tuple(jax.ShapeDtypeStruct(shape, jnp.float32) for shape in shapes),
        scratch_shapes=[pltpu.VMEM((4, CH, CH), jnp.float32)] * 3
        + [pltpu.VMEM(shape, jnp.float32) for shape in shapes]
        + [pltpu.SemaphoreType.DMA((3, 4))],
        compiler_params=pltpu.CompilerParams(vmem_limit_bytes=16 * MIB),
        name="moments",
    )(cohesion.reshape(1, RUNS), rolling.reshape(1, RUNS), x.reshape(RUNS, CH, CH))


def exchange(x, axis, groups=None):
    return lax.all_to_all(
        x, axis, split_axis=0, concat_axis=0, tiled=True, axis_index_groups=groups
    )


def per_device(samples, cohesion, rolling):
    series = exchange(pack(samples).reshape(64, 64, 128), "tm")
    bins = dft(series.reshape(64, 2, 2, 2, 8, 128))
    band = exchange(bins.reshape(64, 64, 128), "tm")
    gathered = exchange(cross(band), "runs", [RING])
    return moments(cohesion, rolling, gathered)


def solution(mesh):
    return jax.shard_map(
        per_device,
        mesh=mesh,
        in_specs=(P("runs", "tm", None), P(), P()),
        out_specs=(
            P(None, "tm", None, None, None),
            P(None, "tm", None, None),
            P(None, "tm", None, None, None),
        ),
        check_vma=False,
    )
```

```python
import functools
import math

import jax
import jax.numpy as jnp
import ml_dtypes
import numpy as np
from jax import lax
from jax.experimental import pallas as pl
from jax.experimental.pallas import tpu as pltpu
from jax.sharding import PartitionSpec as P

CH = 128
BIN = 1024
NC = 4
NQ = 4
TOTAL = 131072
RUNS = 16
NB = 64
T1 = 512
T2 = 256

NT = (((1,), (1,)), ((), ()))
MIB = 1 << 20
PITCH = 72
STEP = 136


def split_table(table):
    high = table.astype(ml_dtypes.bfloat16)
    low = (table - high.astype(np.float64)).astype(ml_dtypes.bfloat16)
    return high, low


@functools.lru_cache(maxsize=None)
def tables():
    even, odd = np.arange(0, 256, 2), np.arange(1, 256, 2)
    t1 = np.arange(256)

    def trig(k, t, period):
        angle = 2.0 * np.pi * (k[:, None] * t[None, :] % period) / period
        return np.cos(angle), np.sin(angle)

    cos_e, sin_e = trig(even, t1, T1)
    cos_o, sin_o = trig(odd, t1, T1)
    sin_e[0] = -np.cos(np.pi * (t1 % 2))
    first_even = np.concatenate([cos_e, -sin_e], axis=0)
    first_odd = np.concatenate([cos_o, -sin_o], axis=0)
    t2 = np.arange(T2)
    cos_t, sin_t = trig(np.concatenate([even, odd]), t2, TOTAL)
    near = np.arange(128)
    second = np.zeros((2, NB, 2, 2, 2, 128))
    edge = np.zeros((NB, 8, T2))
    for band in range(NB):
        for parity in range(2):
            for m, (k2, sign) in enumerate(
                [(2 * band + parity, 1.0), (254 + parity - 2 * band, -1.0)]
            ):
                a = 2.0 * np.pi * (k2 * near % T2) / T2
                second[parity, band, 0, m, 0] = np.cos(a)
                second[parity, band, 0, m, 1] = np.sin(a)
                second[parity, band, 1, m, 0] = -sign * np.sin(a)
                second[parity, band, 1, m, 1] = sign * np.cos(a)
        for half in range(2):
            for m in range(2):
                a = 2.0 * np.pi * ((2 * (2 * band + m) + half) * t2 % 512) / 512
                edge[band, 4 * half + m] = np.cos(a)
                edge[band, 4 * half + 2 + m] = -np.sin(a)
    t = np.arange(TOTAL).reshape(T1, T2)
    window = 0.5 - 0.5 * np.cos(2.0 * np.pi * t / TOTAL)

    def passes(table):
        high, low = split_table(table)
        return np.concatenate([high, high, low], axis=1)

    return (
        window.astype(np.float32),
        cos_t.astype(np.float32),
        sin_t.astype(np.float32),
        passes(first_even),
        passes(first_odd),
        passes(second[0].reshape(256, 256)),
        passes(second[1].reshape(256, 256)),
        passes(edge.reshape(NB * 8, T2)),
    )


def split(value):
    high = value.astype(jnp.bfloat16)
    low = (value - high.astype(jnp.float32)).astype(jnp.bfloat16)
    return high, low


def dot(a, b):
    return jnp.dot(a, b, preferred_element_type=jnp.float32)


def dot_nt(a, b):
    return lax.dot_general(a, b, NT, preferred_element_type=jnp.float32)


def pack_kernel(x_hbm, o_ref, landed, turned, sems):
    copies = [
        pltpu.make_async_copy(x_hbm.at[r, :, h], landed.at[r, h], sems.at[r, h])
        for r in range(2)
        for h in range(2)
    ]
    for copy in copies:
        copy.start()
    for r in range(2):
        for h in range(2):
            copies[2 * r + h].wait()
            for u in range(8):
                turned[r, h, u * STEP : u * STEP + 128, :] = landed[r, h, u].T
            for ch in range(CH):
                o_ref[ch % 64, ch // 64, r, h] = turned[r, h, pl.ds(ch, 8, stride=STEP), :]


def pack(samples):
    x = samples.reshape(2, 8, 2, 128, CH)
    return pl.pallas_call(
        pack_kernel,
        in_specs=[pl.BlockSpec(memory_space=pltpu.HBM)],
        out_specs=pl.BlockSpec(memory_space=pltpu.VMEM),
        out_shape=jax.ShapeDtypeStruct((64, 2, 2, 2, 8, 128), jnp.float32),
        scratch_shapes=[
            pltpu.VMEM((2, 2, 8, 128, CH), jnp.float32),
            pltpu.VMEM((2, 2, 9 * STEP, 128), jnp.float32),
            pltpu.SemaphoreType.DMA((2, 2)),
        ],
        compiler_params=pltpu.CompilerParams(vmem_limit_bytes=50 * MIB),
        name="pack",
    )(x)


def dft_kernel(
    x_ref, w_ref, c_ref, s_ref, fe_ref, fo_ref, se_ref, so_ref, edge_ref, o_ref, edge_in, middle
):
    edge_in[...] = jnp.zeros_like(edge_in)
    first_row = lax.broadcasted_iota(jnp.int32, (256, T2), 0) == 0
    upper = lax.broadcasted_iota(jnp.int32, (32, 8, 128), 1) < 4

    for i in range(4):
        halves = [x_ref[:, i // 2, i % 2, h].reshape(T1, 128) for h in range(2)]
        x = jnp.concatenate(halves, axis=1) * w_ref[...]
        xh, xl = split(x[:256] + x[256:])
        a_even = dot(fe_ref[...], jnp.concatenate([xh, xl, xh], axis=0))
        xh, xl = split(x[:256] - x[256:])
        a_odd = dot(fo_ref[...], jnp.concatenate([xh, xl, xh], axis=0))
        a_re = jnp.concatenate([a_even[:128], a_odd[:128]], axis=0)
        a_im = jnp.concatenate([a_even[128:], a_odd[128:]], axis=0)
        c, s = c_ref[...], s_ref[...]
        b_re = a_re * c + a_im * s
        b_im = a_im * c - a_re * s
        edge_in[i : i + 1, :] = b_re[:1]
        edge_in[i + 4 : i + 5, :] = b_im[:1]
        b_re = jnp.where(first_row, 0.0, b_re)
        b_im = jnp.where(first_row, 0.0, b_im)
        plus = jnp.concatenate(
            [b_re[:, :128] + b_re[:, 128:], b_im[:, :128] + b_im[:, 128:]], axis=1
        )
        minus = jnp.concatenate(
            [b_re[:, :128] - b_re[:, 128:], b_im[:, :128] - b_im[:, 128:]], axis=1
        )
        middle[i, 0, 0], middle[i, 0, 1] = split(plus)
        middle[i, 1, 0], middle[i, 1, 1] = split(minus)

    eh, el = split(edge_in[...])
    edge = dot_nt(edge_ref[...], jnp.concatenate([eh, el, eh], axis=1))
    first_lane = lax.broadcasted_iota(jnp.int32, (512, 128), 1) == 0
    sub = lax.broadcasted_iota(jnp.int32, (512, 128), 0) % 8 < 4

    for i in range(4):
        bh, bl = middle[i, 0, 0], middle[i, 0, 1]
        o_even = dot_nt(se_ref[:, :256], bl) + dot_nt(
            se_ref[:, 256:], jnp.concatenate([bh, bh], axis=1)
        )
        bh, bl = middle[i, 1, 0], middle[i, 1, 1]
        o_odd = dot_nt(so_ref[:, :256], bl) + dot_nt(
            so_ref[:, 256:], jnp.concatenate([bh, bh], axis=1)
        )
        low = edge if i == 0 else pltpu.roll(edge, 128 - i, 1)
        extra = jnp.where(sub, low, pltpu.roll(edge, 124 - i, 1))
        extra = jnp.where(first_lane, extra, 0.0).reshape(32, 2, 8, 128)
        for half in range(2):
            lanes = slice(128 * half, 128 * half + 128)
            e = o_even[:, lanes].reshape(32, 8, 128)
            o = o_odd[:, lanes].reshape(32, 8, 128)
            first = jnp.where(upper, e, pltpu.roll(o, 4, 1))
            second = jnp.where(upper, pltpu.roll(e, 4, 1), o)
            o_ref[:, 0, i, half] = first + extra[:, 0] if half == 0 else first
            o_ref[:, 1, i, half] = second + extra[:, 1] if half == 0 else second


def dft(x):
    consts = [jnp.asarray(t) for t in tables()]
    vmem = pl.BlockSpec(memory_space=pltpu.VMEM)
    return pl.pallas_call(
        dft_kernel,
        in_specs=[vmem] * (1 + len(consts)),
        out_specs=vmem,
        out_shape=jax.ShapeDtypeStruct((NB // 2, 2, 4, 2, 8, 128), jnp.float32),
        scratch_shapes=[
            pltpu.VMEM((128, T2), jnp.float32),
            pltpu.VMEM((4, 2, 2, 256, 256), jnp.bfloat16),
        ],
        compiler_params=pltpu.CompilerParams(vmem_limit_bytes=24 * MIB),
        name="dft",
    )(x, *consts)


def cross_kernel(x_ref, o_ref, rows, *, scale):
    row = lax.broadcasted_iota(jnp.int32, (CH, CH), 0)
    col = lax.broadcasted_iota(jnp.int32, (CH, CH), 1)
    for q in range(64):
        rows[q * PITCH : q * PITCH + 64, :] = x_ref[q * 64 : q * 64 + 64, :]
    for r in range(2):
        parts = []
        for part in range(2):
            for c in range(2):
                cols = [
                    rows[pl.ds((c * 2 + r) * 16 + half * 8 + part * 2 + m, 64, stride=PITCH), :]
                    for m in (0, 1, 4, 5)
                    for half in range(2)
                ]
                parts.append(jnp.concatenate(cols, axis=1))
        v = jnp.concatenate(parts, axis=0)
        vh, vl = split(v)
        mixed = dot_nt(vh, vl)
        g = dot_nt(vh, vh) + (mixed + mixed.T)
        real = g[:CH, :CH] + g[CH:, CH:]
        imag = g[CH:, :CH] - g[:CH, CH:]
        packed = jnp.where(row >= col, real, imag) * scale
        for y in range(8):
            o_ref[y, r] = packed


def cross(x):
    scale = 1.0 / (0.375 * BIN * TOTAL)
    return pl.pallas_call(
        functools.partial(cross_kernel, scale=scale),
        in_specs=[pl.BlockSpec(memory_space=pltpu.VMEM)],
        out_specs=pl.BlockSpec(memory_space=pltpu.VMEM),
        out_shape=jax.ShapeDtypeStruct((8, 2, CH, CH), jnp.float32),
        scratch_shapes=[pltpu.VMEM((65 * PITCH, 128), jnp.float32)],
        compiler_params=pltpu.CompilerParams(vmem_limit_bytes=24 * MIB),
        name="cross",
    )(x.reshape(64 * 64, 128))


def moments_kernel(
    lev_vec, roll_vec, x_ref, lm_hbm, sp_hbm, rm_hbm, sums, rolls, squares, lm, sp, rm, sems
):
    row = lax.broadcasted_iota(jnp.int32, (CH, CH), 0)
    col = lax.broadcasted_iota(jnp.int32, (CH, CH), 1)
    levels, turns = lev_vec[...], roll_vec[...]
    lev_ref = [levels[0, r] for r in range(RUNS)]
    roll_ref = [turns[0, r] for r in range(RUNS)]
    sums[...] = jnp.zeros_like(sums)
    rolls[...] = jnp.zeros_like(rolls)
    squares[...] = jnp.zeros_like(squares)

    def unpack(m):
        t = m.T
        real = jnp.where(row >= col, m, t)
        imag = jnp.where(row < col, m, jnp.where(row > col, -t, 0.0))
        return real, imag

    def count(values, level):
        total = jnp.sum((values == level).astype(jnp.float32), axis=1, keepdims=True)
        return jnp.maximum(total, 1.0)

    sends = []

    def send(source, target, kind, level):
        copy = pltpu.make_async_copy(source.at[level], target.at[level], sems.at[kind, level])
        copy.start()
        sends.append(copy)

    for r in range(RUNS):
        value = x_ref[r]
        rolls[roll_ref[r]] += value
        sums[lev_ref[r]] += value
    for q in range(NQ):
        rm[q, 0, 0], rm[q, 0, 1] = unpack(rolls[q] / count(turns, q))
        send(rm, rm_hbm, 0, q)
    for l in range(NC):
        mean = sums[l] / count(levels, l)
        sums[l] = mean
        lm[l, 0, 0], lm[l, 0, 1] = unpack(mean)
        send(lm, lm_hbm, 1, l)
    for r in range(RUNS):
        level = lev_ref[r]
        offset = x_ref[r] - sums[level]
        squares[level] += offset * offset
    for l in range(NC):
        s = squares[l]
        sp[l, 0] = BIN * jnp.where(row == col, s, s + s.T)
        send(sp, sp_hbm, 2, l)
    for copy in sends:
        copy.wait()


def moments(cohesion, rolling, x):
    vmem = pl.BlockSpec(memory_space=pltpu.VMEM)
    smem = pl.BlockSpec(memory_space=pltpu.SMEM)
    hbm = pl.BlockSpec(memory_space=pltpu.HBM)
    shapes = [(NC, 1, 2, CH, CH), (NC, 1, CH, CH), (NQ, 1, 2, CH, CH)]
    return pl.pallas_call(
        moments_kernel,
        in_specs=[vmem, vmem, vmem],
        out_specs=(hbm, hbm, hbm),
        out_shape=tuple(jax.ShapeDtypeStruct(shape, jnp.float32) for shape in shapes),
        scratch_shapes=[pltpu.VMEM((4, CH, CH), jnp.float32)] * 3
        + [pltpu.VMEM(shape, jnp.float32) for shape in shapes]
        + [pltpu.SemaphoreType.DMA((3, 4))],
        compiler_params=pltpu.CompilerParams(vmem_limit_bytes=16 * MIB),
        name="moments",
    )(cohesion.reshape(1, RUNS), rolling.reshape(1, RUNS), x.reshape(RUNS, CH, CH))


def exchange(x, axis):
    return lax.all_to_all(x, axis, split_axis=0, concat_axis=0, tiled=True)


def per_device(samples, cohesion, rolling):
    series = exchange(pack(samples).reshape(64, 64, 128), "tm")
    bins = dft(series.reshape(64, 2, 2, 2, 8, 128))
    band = exchange(bins.reshape(64, 64, 128), "tm")
    gathered = exchange(cross(band), "runs")
    return moments(cohesion, rolling, gathered)


def solution(mesh):
    return jax.shard_map(
        per_device,
        mesh=mesh,
        in_specs=(P("runs", "tm", None), P(), P()),
        out_specs=(
            P(None, "tm", None, None, None),
            P(None, "tm", None, None),
            P(None, "tm", None, None, None),
        ),
        check_vma=False,
    )
```

```python
import functools
import math

import jax
import jax.numpy as jnp
import ml_dtypes
import numpy as np
from jax import lax
from jax.experimental import pallas as pl
from jax.experimental.pallas import tpu as pltpu
from jax.sharding import PartitionSpec as P

CH = 128
BIN = 1024
NC = 4
NQ = 4
TOTAL = 131072
RUNS = 16
NB = 64
T1 = 512
T2 = 256

NT = (((1,), (1,)), ((), ()))
MIB = 1 << 20
PITCH = 136
STEP = 136


def split_table(table):
    high = table.astype(ml_dtypes.bfloat16)
    low = (table - high.astype(np.float64)).astype(ml_dtypes.bfloat16)
    return high, low


@functools.lru_cache(maxsize=None)
def tables():
    even, odd = np.arange(0, 256, 2), np.arange(1, 256, 2)
    t1 = np.arange(256)

    def trig(k, t, period):
        angle = 2.0 * np.pi * (k[:, None] * t[None, :] % period) / period
        return np.cos(angle), np.sin(angle)

    cos_e, sin_e = trig(even, t1, T1)
    cos_o, sin_o = trig(odd, t1, T1)
    sin_e[0] = -np.cos(np.pi * (t1 % 2))
    first_even = np.concatenate([cos_e, -sin_e], axis=0)
    first_odd = np.concatenate([cos_o, -sin_o], axis=0)
    t2 = np.arange(T2)
    cos_t, sin_t = trig(np.concatenate([even, odd]), t2, TOTAL)
    near = np.arange(128)
    second = np.zeros((2, NB, 2, 2, 2, 128))
    edge = np.zeros((NB, 8, T2))
    for band in range(NB):
        for parity in range(2):
            for m, (k2, sign) in enumerate(
                [(2 * band + parity, 1.0), (254 + parity - 2 * band, -1.0)]
            ):
                a = 2.0 * np.pi * (k2 * near % T2) / T2
                second[parity, band, 0, m, 0] = np.cos(a)
                second[parity, band, 0, m, 1] = np.sin(a)
                second[parity, band, 1, m, 0] = -sign * np.sin(a)
                second[parity, band, 1, m, 1] = sign * np.cos(a)
        for half in range(2):
            for m in range(2):
                a = 2.0 * np.pi * ((2 * (2 * band + m) + half) * t2 % 512) / 512
                edge[band, 4 * half + m] = np.cos(a)
                edge[band, 4 * half + 2 + m] = -np.sin(a)
    t = np.arange(TOTAL).reshape(T1, T2)
    window = 0.5 - 0.5 * np.cos(2.0 * np.pi * t / TOTAL)

    def passes(table):
        high, low = split_table(table)
        return np.concatenate([high, high, low], axis=1)

    return (
        window.astype(np.float32),
        cos_t.astype(np.float32),
        sin_t.astype(np.float32),
        passes(first_even),
        passes(first_odd),
        passes(second[0].reshape(256, 256)),
        passes(second[1].reshape(256, 256)),
        passes(edge.reshape(NB * 8, T2)),
    )


def split(value):
    high = value.astype(jnp.bfloat16)
    low = (value - high.astype(jnp.float32)).astype(jnp.bfloat16)
    return high, low


def dot(a, b):
    return jnp.dot(a, b, preferred_element_type=jnp.float32)


def dot_nt(a, b):
    return lax.dot_general(a, b, NT, preferred_element_type=jnp.float32)


def pack_kernel(x_hbm, o_ref, landed, turned, sems):
    copies = [
        pltpu.make_async_copy(x_hbm.at[r, :, h], landed.at[r, h], sems.at[r, h])
        for r in range(2)
        for h in range(2)
    ]
    for copy in copies:
        copy.start()
    for r in range(2):
        for h in range(2):
            copies[2 * r + h].wait()
            for u in range(8):
                turned[r, h, u * STEP : u * STEP + 128, :] = landed[r, h, u].T
            for ch in range(CH):
                o_ref[ch % 32, r, ch // 32, h] = turned[r, h, pl.ds(ch, 8, stride=STEP), :]


def pack(samples):
    x = samples.reshape(2, 8, 2, 128, CH)
    return pl.pallas_call(
        pack_kernel,
        in_specs=[pl.BlockSpec(memory_space=pltpu.HBM)],
        out_specs=pl.BlockSpec(memory_space=pltpu.VMEM),
        out_shape=jax.ShapeDtypeStruct((32, 2, 4, 2, 8, 128), jnp.float32),
        scratch_shapes=[
            pltpu.VMEM((2, 2, 8, 128, CH), jnp.float32),
            pltpu.VMEM((2, 2, 9 * STEP, 128), jnp.float32),
            pltpu.SemaphoreType.DMA((2, 2)),
        ],
        compiler_params=pltpu.CompilerParams(vmem_limit_bytes=50 * MIB),
        name="pack",
    )(x)


def dft_kernel(
    x_ref, w_ref, c_ref, s_ref, fe_ref, fo_ref, se_ref, so_ref, edge_ref, o_ref, edge_in, middle
):
    edge_in[...] = jnp.zeros_like(edge_in)
    first_row = lax.broadcasted_iota(jnp.int32, (256, T2), 0) == 0
    upper = lax.broadcasted_iota(jnp.int32, (32, 8, 128), 1) < 4

    for i in range(4):
        halves = [x_ref[:, i, h].reshape(T1, 128) for h in range(2)]
        x = jnp.concatenate(halves, axis=1) * w_ref[...]
        xh, xl = split(x[:256] + x[256:])
        a_even = dot(fe_ref[...], jnp.concatenate([xh, xl, xh], axis=0))
        xh, xl = split(x[:256] - x[256:])
        a_odd = dot(fo_ref[...], jnp.concatenate([xh, xl, xh], axis=0))
        a_re = jnp.concatenate([a_even[:128], a_odd[:128]], axis=0)
        a_im = jnp.concatenate([a_even[128:], a_odd[128:]], axis=0)
        c, s = c_ref[...], s_ref[...]
        b_re = a_re * c + a_im * s
        b_im = a_im * c - a_re * s
        edge_in[i : i + 1, :] = b_re[:1]
        edge_in[i + 4 : i + 5, :] = b_im[:1]
        b_re = jnp.where(first_row, 0.0, b_re)
        b_im = jnp.where(first_row, 0.0, b_im)
        plus = jnp.concatenate(
            [b_re[:, :128] + b_re[:, 128:], b_im[:, :128] + b_im[:, 128:]], axis=1
        )
        minus = jnp.concatenate(
            [b_re[:, :128] - b_re[:, 128:], b_im[:, :128] - b_im[:, 128:]], axis=1
        )
        middle[i, 0, 0], middle[i, 0, 1] = split(plus)
        middle[i, 1, 0], middle[i, 1, 1] = split(minus)

    eh, el = split(edge_in[...])
    edge = dot_nt(edge_ref[...], jnp.concatenate([eh, el, eh], axis=1))
    first_lane = lax.broadcasted_iota(jnp.int32, (512, 128), 1) == 0
    sub = lax.broadcasted_iota(jnp.int32, (512, 128), 0) % 8 < 4

    for i in range(4):
        bh, bl = middle[i, 0, 0], middle[i, 0, 1]
        o_even = dot_nt(se_ref[:, :256], bl) + dot_nt(
            se_ref[:, 256:], jnp.concatenate([bh, bh], axis=1)
        )
        bh, bl = middle[i, 1, 0], middle[i, 1, 1]
        o_odd = dot_nt(so_ref[:, :256], bl) + dot_nt(
            so_ref[:, 256:], jnp.concatenate([bh, bh], axis=1)
        )
        low = edge if i == 0 else pltpu.roll(edge, 128 - i, 1)
        extra = jnp.where(sub, low, pltpu.roll(edge, 124 - i, 1))
        extra = jnp.where(first_lane, extra, 0.0).reshape(32, 2, 8, 128)
        for half in range(2):
            lanes = slice(128 * half, 128 * half + 128)
            e = o_even[:, lanes].reshape(32, 8, 128)
            o = o_odd[:, lanes].reshape(32, 8, 128)
            first = jnp.where(upper, e, pltpu.roll(o, 4, 1))
            second = jnp.where(upper, pltpu.roll(e, 4, 1), o)
            o_ref[:, 0, i, half] = first + extra[:, 0] if half == 0 else first
            o_ref[:, 1, i, half] = second + extra[:, 1] if half == 0 else second


def dft(x):
    consts = [jnp.asarray(t) for t in tables()]
    vmem = pl.BlockSpec(memory_space=pltpu.VMEM)
    return pl.pallas_call(
        dft_kernel,
        in_specs=[vmem] * (1 + len(consts)),
        out_specs=vmem,
        out_shape=jax.ShapeDtypeStruct((NB // 2, 2, 4, 2, 8, 128), jnp.float32),
        scratch_shapes=[
            pltpu.VMEM((128, T2), jnp.float32),
            pltpu.VMEM((4, 2, 2, 256, 256), jnp.bfloat16),
        ],
        compiler_params=pltpu.CompilerParams(vmem_limit_bytes=24 * MIB),
        name="dft",
    )(x, *consts)


def cross_kernel(x_ref, o_ref, rows, *, scale):
    row = lax.broadcasted_iota(jnp.int32, (CH, CH), 0)
    col = lax.broadcasted_iota(jnp.int32, (CH, CH), 1)
    for chip in range(32):
        rows[chip * PITCH : chip * PITCH + 128, :] = x_ref[chip * 128 : chip * 128 + 128, :]
    for band in range(2):
        parts = []
        for part in range(2):
            for c in range(4):
                cols = [
                    rows[pl.ds((band * 4 + c) * 16 + half * 8 + part * 2 + m, 32, stride=PITCH), :]
                    for m in (0, 1, 4, 5)
                    for half in range(2)
                ]
                parts.append(jnp.concatenate(cols, axis=1))
        v = jnp.concatenate(parts, axis=0)
        vh, vl = split(v)
        mixed = dot_nt(vh, vl)
        g = dot_nt(vh, vh) + (mixed + mixed.T)
        real = g[:CH, :CH] + g[CH:, CH:]
        imag = g[CH:, :CH] - g[:CH, CH:]
        packed = jnp.where(row >= col, real, imag) * scale
        for y in range(8):
            o_ref[band * 8 + y] = packed


def cross(x):
    scale = 1.0 / (0.375 * BIN * TOTAL)
    return pl.pallas_call(
        functools.partial(cross_kernel, scale=scale),
        in_specs=[pl.BlockSpec(memory_space=pltpu.VMEM)],
        out_specs=pl.BlockSpec(memory_space=pltpu.VMEM),
        out_shape=jax.ShapeDtypeStruct((16, CH, CH), jnp.float32),
        scratch_shapes=[pltpu.VMEM((33 * PITCH, 128), jnp.float32)],
        compiler_params=pltpu.CompilerParams(vmem_limit_bytes=24 * MIB),
        name="cross",
    )(x.reshape(64 * 64, 128))


def moments_kernel(
    lev_vec, roll_vec, x_ref, lm_hbm, sp_hbm, rm_hbm, sums, rolls, squares, lm, sp, rm, sems
):
    row = lax.broadcasted_iota(jnp.int32, (CH, CH), 0)
    col = lax.broadcasted_iota(jnp.int32, (CH, CH), 1)
    levels, turns = lev_vec[...], roll_vec[...]
    order = [2 * (k % 8) + k // 8 for k in range(RUNS)]
    lev_ref = [levels[0, r] for r in order]
    roll_ref = [turns[0, r] for r in order]
    sums[...] = jnp.zeros_like(sums)
    rolls[...] = jnp.zeros_like(rolls)
    squares[...] = jnp.zeros_like(squares)

    def unpack(m):
        t = m.T
        real = jnp.where(row >= col, m, t)
        imag = jnp.where(row < col, m, jnp.where(row > col, -t, 0.0))
        return real, imag

    def count(values, level):
        total = jnp.sum((values == level).astype(jnp.float32), axis=1, keepdims=True)
        return jnp.maximum(total, 1.0)

    sends = []

    def send(source, target, kind, level):
        copy = pltpu.make_async_copy(source.at[level], target.at[level], sems.at[kind, level])
        copy.start()
        sends.append(copy)

    for r in range(RUNS):
        value = x_ref[r]
        rolls[roll_ref[r]] += value
        sums[lev_ref[r]] += value
    for q in range(NQ):
        rm[q, 0, 0], rm[q, 0, 1] = unpack(rolls[q] / count(turns, q))
        send(rm, rm_hbm, 0, q)
    for l in range(NC):
        mean = sums[l] / count(levels, l)
        sums[l] = mean
        lm[l, 0, 0], lm[l, 0, 1] = unpack(mean)
        send(lm, lm_hbm, 1, l)
    for r in range(RUNS):
        level = lev_ref[r]
        offset = x_ref[r] - sums[level]
        squares[level] += offset * offset
    for l in range(NC):
        s = squares[l]
        sp[l, 0] = BIN * jnp.where(row == col, s, s + s.T)
        send(sp, sp_hbm, 2, l)
    for copy in sends:
        copy.wait()


def moments(cohesion, rolling, x):
    vmem = pl.BlockSpec(memory_space=pltpu.VMEM)
    smem = pl.BlockSpec(memory_space=pltpu.SMEM)
    hbm = pl.BlockSpec(memory_space=pltpu.HBM)
    shapes = [(NC, 1, 2, CH, CH), (NC, 1, CH, CH), (NQ, 1, 2, CH, CH)]
    return pl.pallas_call(
        moments_kernel,
        in_specs=[vmem, vmem, vmem],
        out_specs=(hbm, hbm, hbm),
        out_shape=tuple(jax.ShapeDtypeStruct(shape, jnp.float32) for shape in shapes),
        scratch_shapes=[pltpu.VMEM((4, CH, CH), jnp.float32)] * 3
        + [pltpu.VMEM(shape, jnp.float32) for shape in shapes]
        + [pltpu.SemaphoreType.DMA((3, 4))],
        compiler_params=pltpu.CompilerParams(vmem_limit_bytes=16 * MIB),
        name="moments",
    )(cohesion.reshape(1, RUNS), rolling.reshape(1, RUNS), x)


def exchange(x, axis, groups=None):
    return lax.all_to_all(
        x, axis, split_axis=0, concat_axis=0, tiled=True, axis_index_groups=groups
    )


def per_device(samples, cohesion, rolling):
    same_core = [[2 * chip + core for chip in range(32)] for core in range(2)]
    column = [[16 * chip + k for k in range(16)] for chip in range(32)]
    series = exchange(pack(samples).reshape(64, 64, 128), "tm")
    bins = dft(series.reshape(64, 4, 2, 8, 128))
    bands = exchange(bins.reshape(32, 128, 128), "tm", same_core)
    gathered = exchange(cross(bands), ("tm", "runs"), column)
    return moments(cohesion, rolling, gathered)


def solution(mesh):
    return jax.shard_map(
        per_device,
        mesh=mesh,
        in_specs=(P("runs", "tm", None), P(), P()),
        out_specs=(
            P(None, "tm", None, None, None),
            P(None, "tm", None, None),
            P(None, "tm", None, None, None),
        ),
        check_vma=False,
    )
```

```python
import functools
import math

import jax
import jax.numpy as jnp
import ml_dtypes
import numpy as np
from jax import lax
from jax.experimental import pallas as pl
from jax.experimental.pallas import tpu as pltpu
from jax.sharding import PartitionSpec as P

CH = 128
BIN = 1024
NC = 4
NQ = 4
TOTAL = 131072
RUNS = 16
NB = 64
T1 = 512
T2 = 256

NT = (((1,), (1,)), ((), ()))
MIB = 1 << 20
PITCH = 136
STEP = 136


def split_table(table):
    high = table.astype(ml_dtypes.bfloat16)
    low = (table - high.astype(np.float64)).astype(ml_dtypes.bfloat16)
    return high, low


@functools.lru_cache(maxsize=None)
def tables():
    even, odd = np.arange(0, 256, 2), np.arange(1, 256, 2)
    t1 = np.arange(256)

    def trig(k, t, period):
        angle = 2.0 * np.pi * (k[:, None] * t[None, :] % period) / period
        return np.cos(angle), np.sin(angle)

    cos_e, sin_e = trig(even, t1, T1)
    cos_o, sin_o = trig(odd, t1, T1)
    sin_e[0] = -np.cos(np.pi * (t1 % 2))
    first_even = np.concatenate([cos_e, -sin_e], axis=0)
    first_odd = np.concatenate([cos_o, -sin_o], axis=0)
    t2 = np.arange(T2)
    cos_t, sin_t = trig(np.concatenate([even, odd]), t2, TOTAL)
    near = np.arange(128)
    second = np.zeros((2, NB, 2, 2, 2, 128))
    edge = np.zeros((NB, 8, T2))
    for band in range(NB):
        for parity in range(2):
            for m, (k2, sign) in enumerate(
                [(2 * band + parity, 1.0), (254 + parity - 2 * band, -1.0)]
            ):
                a = 2.0 * np.pi * (k2 * near % T2) / T2
                second[parity, band, 0, m, 0] = np.cos(a)
                second[parity, band, 0, m, 1] = np.sin(a)
                second[parity, band, 1, m, 0] = -sign * np.sin(a)
                second[parity, band, 1, m, 1] = sign * np.cos(a)
        for half in range(2):
            for m in range(2):
                a = 2.0 * np.pi * ((2 * (2 * band + m) + half) * t2 % 512) / 512
                edge[band, 4 * half + m] = np.cos(a)
                edge[band, 4 * half + 2 + m] = -np.sin(a)
    t = np.arange(TOTAL).reshape(T1, T2)
    window = 0.5 - 0.5 * np.cos(2.0 * np.pi * t / TOTAL)

    def passes(table):
        high, low = split_table(table)
        return np.concatenate([high, high, low], axis=1)

    return (
        window.astype(np.float32),
        cos_t.astype(np.float32),
        sin_t.astype(np.float32),
        passes(first_even),
        passes(first_odd),
        passes(second[0].reshape(256, 256)),
        passes(second[1].reshape(256, 256)),
        passes(edge.reshape(NB * 8, T2)),
    )


def split(value):
    high = value.astype(jnp.bfloat16)
    low = (value - high.astype(jnp.float32)).astype(jnp.bfloat16)
    return high, low


def dot(a, b):
    return jnp.dot(a, b, preferred_element_type=jnp.float32)


def dot_nt(a, b):
    return lax.dot_general(a, b, NT, preferred_element_type=jnp.float32)


def pack_kernel(x_hbm, o_ref, landed, turned, sems):
    copies = [
        pltpu.make_async_copy(x_hbm.at[r, :, h], landed.at[r, h], sems.at[r, h])
        for r in range(2)
        for h in range(2)
    ]
    for copy in copies:
        copy.start()
    for r in range(2):
        for h in range(2):
            copies[2 * r + h].wait()
            for u in range(8):
                turned[r, h, u * STEP : u * STEP + 128, :] = landed[r, h, u].T
            for ch in range(CH):
                o_ref[ch % 32, r, ch // 32, h] = turned[r, h, pl.ds(ch, 8, stride=STEP), :]


def pack(samples):
    x = samples.reshape(2, 8, 2, 128, CH)
    return pl.pallas_call(
        pack_kernel,
        in_specs=[pl.BlockSpec(memory_space=pltpu.HBM)],
        out_specs=pl.BlockSpec(memory_space=pltpu.VMEM),
        out_shape=jax.ShapeDtypeStruct((32, 2, 4, 2, 8, 128), jnp.float32),
        scratch_shapes=[
            pltpu.VMEM((2, 2, 8, 128, CH), jnp.float32),
            pltpu.VMEM((2, 2, 9 * STEP, 128), jnp.float32),
            pltpu.SemaphoreType.DMA((2, 2)),
        ],
        compiler_params=pltpu.CompilerParams(vmem_limit_bytes=50 * MIB),
        name="pack",
    )(x)


def dft_kernel(
    x_ref, w_ref, c_ref, s_ref, fe_ref, fo_ref, se_ref, so_ref, edge_ref, o_ref, edge_in, middle
):
    edge_in[...] = jnp.zeros_like(edge_in)
    first_row = lax.broadcasted_iota(jnp.int32, (256, T2), 0) == 0
    upper = lax.broadcasted_iota(jnp.int32, (32, 8, 128), 1) < 4

    for i in range(4):
        halves = [x_ref[:, i, h].reshape(T1, 128) for h in range(2)]
        x = jnp.concatenate(halves, axis=1) * w_ref[...]
        xh, xl = split(x[:256] + x[256:])
        a_even = dot(fe_ref[:, :256], xl) + dot(
            fe_ref[:, 256:], jnp.concatenate([xh, xh], axis=0)
        )
        xh, xl = split(x[:256] - x[256:])
        a_odd = dot(fo_ref[:, :256], xl) + dot(
            fo_ref[:, 256:], jnp.concatenate([xh, xh], axis=0)
        )
        a_re = jnp.concatenate([a_even[:128], a_odd[:128]], axis=0)
        a_im = jnp.concatenate([a_even[128:], a_odd[128:]], axis=0)
        c, s = c_ref[...], s_ref[...]
        b_re = a_re * c + a_im * s
        b_im = a_im * c - a_re * s
        edge_in[i : i + 1, :] = b_re[:1]
        edge_in[i + 4 : i + 5, :] = b_im[:1]
        b_re = jnp.where(first_row, 0.0, b_re)
        b_im = jnp.where(first_row, 0.0, b_im)
        plus = jnp.concatenate(
            [b_re[:, :128] + b_re[:, 128:], b_im[:, :128] + b_im[:, 128:]], axis=1
        )
        minus = jnp.concatenate(
            [b_re[:, :128] - b_re[:, 128:], b_im[:, :128] - b_im[:, 128:]], axis=1
        )
        middle[i, 0, 0], middle[i, 0, 1] = split(plus)
        middle[i, 1, 0], middle[i, 1, 1] = split(minus)

    eh, el = split(edge_in[...])
    edge = dot_nt(edge_ref[...], jnp.concatenate([eh, el, eh], axis=1))
    first_lane = lax.broadcasted_iota(jnp.int32, (512, 128), 1) == 0
    sub = lax.broadcasted_iota(jnp.int32, (512, 128), 0) % 8 < 4

    for i in range(4):
        bh, bl = middle[i, 0, 0], middle[i, 0, 1]
        o_even = dot_nt(se_ref[:, :256], bl) + dot_nt(
            se_ref[:, 256:], jnp.concatenate([bh, bh], axis=1)
        )
        bh, bl = middle[i, 1, 0], middle[i, 1, 1]
        o_odd = dot_nt(so_ref[:, :256], bl) + dot_nt(
            so_ref[:, 256:], jnp.concatenate([bh, bh], axis=1)
        )
        low = edge if i == 0 else pltpu.roll(edge, 128 - i, 1)
        extra = jnp.where(sub, low, pltpu.roll(edge, 124 - i, 1))
        extra = jnp.where(first_lane, extra, 0.0).reshape(32, 2, 8, 128)
        for half in range(2):
            lanes = slice(128 * half, 128 * half + 128)
            e = o_even[:, lanes].reshape(32, 8, 128)
            o = o_odd[:, lanes].reshape(32, 8, 128)
            first = jnp.where(upper, e, pltpu.roll(o, 4, 1))
            second = jnp.where(upper, pltpu.roll(e, 4, 1), o)
            o_ref[:, 0, i, half] = first + extra[:, 0] if half == 0 else first
            o_ref[:, 1, i, half] = second + extra[:, 1] if half == 0 else second


def dft(x):
    consts = [jnp.asarray(t) for t in tables()]
    vmem = pl.BlockSpec(memory_space=pltpu.VMEM)
    return pl.pallas_call(
        dft_kernel,
        in_specs=[vmem] * (1 + len(consts)),
        out_specs=vmem,
        out_shape=jax.ShapeDtypeStruct((NB // 2, 2, 4, 2, 8, 128), jnp.float32),
        scratch_shapes=[
            pltpu.VMEM((128, T2), jnp.float32),
            pltpu.VMEM((4, 2, 2, 256, 256), jnp.bfloat16),
        ],
        compiler_params=pltpu.CompilerParams(vmem_limit_bytes=24 * MIB),
        name="dft",
    )(x, *consts)


def cross_kernel(x_ref, o_ref, rows, *, scale):
    row = lax.broadcasted_iota(jnp.int32, (CH, CH), 0)
    col = lax.broadcasted_iota(jnp.int32, (CH, CH), 1)
    for chip in range(32):
        rows[chip * PITCH : chip * PITCH + 128, :] = x_ref[chip * 128 : chip * 128 + 128, :]
    for band in range(2):
        parts = []
        for part in range(2):
            for c in range(4):
                cols = [
                    rows[pl.ds((band * 4 + c) * 16 + half * 8 + part * 2 + m, 32, stride=PITCH), :]
                    for m in (0, 1, 4, 5)
                    for half in range(2)
                ]
                parts.append(jnp.concatenate(cols, axis=1))
        v = jnp.concatenate(parts, axis=0)
        vh, vl = split(v)
        mixed = dot_nt(vh, vl)
        g = dot_nt(vh, vh) + (mixed + mixed.T)
        real = g[:CH, :CH] + g[CH:, CH:]
        imag = g[CH:, :CH] - g[:CH, CH:]
        packed = jnp.where(row >= col, real, imag) * scale
        for y in range(8):
            o_ref[band * 8 + y] = packed


def cross(x):
    scale = 1.0 / (0.375 * BIN * TOTAL)
    return pl.pallas_call(
        functools.partial(cross_kernel, scale=scale),
        in_specs=[pl.BlockSpec(memory_space=pltpu.VMEM)],
        out_specs=pl.BlockSpec(memory_space=pltpu.VMEM),
        out_shape=jax.ShapeDtypeStruct((16, CH, CH), jnp.float32),
        scratch_shapes=[pltpu.VMEM((33 * PITCH, 128), jnp.float32)],
        compiler_params=pltpu.CompilerParams(vmem_limit_bytes=24 * MIB),
        name="cross",
    )(x.reshape(64 * 64, 128))


def moments_kernel(
    lev_vec, roll_vec, x_ref, lm_hbm, sp_hbm, rm_hbm, sums, rolls, squares, lm, sp, rm, sems
):
    row = lax.broadcasted_iota(jnp.int32, (CH, CH), 0)
    col = lax.broadcasted_iota(jnp.int32, (CH, CH), 1)
    levels, turns = lev_vec[...], roll_vec[...]
    order = [2 * (k % 8) + k // 8 for k in range(RUNS)]
    lev_ref = [levels[0, r] for r in order]
    roll_ref = [turns[0, r] for r in order]
    sums[...] = jnp.zeros_like(sums)
    rolls[...] = jnp.zeros_like(rolls)
    squares[...] = jnp.zeros_like(squares)

    def unpack(m):
        t = m.T
        real = jnp.where(row >= col, m, t)
        imag = jnp.where(row < col, m, jnp.where(row > col, -t, 0.0))
        return real, imag

    def count(values, level):
        total = jnp.sum((values == level).astype(jnp.float32), axis=1, keepdims=True)
        return jnp.maximum(total, 1.0)

    sends = []

    def send(source, target, kind, level):
        copy = pltpu.make_async_copy(source.at[level], target.at[level], sems.at[kind, level])
        copy.start()
        sends.append(copy)

    for r in range(RUNS):
        value = x_ref[r]
        rolls[roll_ref[r]] += value
        sums[lev_ref[r]] += value
    for q in range(NQ):
        rm[q, 0, 0], rm[q, 0, 1] = unpack(rolls[q] / count(turns, q))
        send(rm, rm_hbm, 0, q)
    for l in range(NC):
        mean = sums[l] / count(levels, l)
        sums[l] = mean
        lm[l, 0, 0], lm[l, 0, 1] = unpack(mean)
        send(lm, lm_hbm, 1, l)
    for r in range(RUNS):
        level = lev_ref[r]
        offset = x_ref[r] - sums[level]
        squares[level] += offset * offset
    for l in range(NC):
        s = squares[l]
        sp[l, 0] = BIN * jnp.where(row == col, s, s + s.T)
        send(sp, sp_hbm, 2, l)
    for copy in sends:
        copy.wait()


def moments(cohesion, rolling, x):
    vmem = pl.BlockSpec(memory_space=pltpu.VMEM)
    smem = pl.BlockSpec(memory_space=pltpu.SMEM)
    hbm = pl.BlockSpec(memory_space=pltpu.HBM)
    shapes = [(NC, 1, 2, CH, CH), (NC, 1, CH, CH), (NQ, 1, 2, CH, CH)]
    return pl.pallas_call(
        moments_kernel,
        in_specs=[vmem, vmem, vmem],
        out_specs=(hbm, hbm, hbm),
        out_shape=tuple(jax.ShapeDtypeStruct(shape, jnp.float32) for shape in shapes),
        scratch_shapes=[pltpu.VMEM((4, CH, CH), jnp.float32)] * 3
        + [pltpu.VMEM(shape, jnp.float32) for shape in shapes]
        + [pltpu.SemaphoreType.DMA((3, 4))],
        compiler_params=pltpu.CompilerParams(vmem_limit_bytes=16 * MIB),
        name="moments",
    )(cohesion.reshape(1, RUNS), rolling.reshape(1, RUNS), x)


def exchange(x, axis, groups=None):
    return lax.all_to_all(
        x, axis, split_axis=0, concat_axis=0, tiled=True, axis_index_groups=groups
    )


def per_device(samples, cohesion, rolling):
    same_core = [[2 * chip + core for chip in range(32)] for core in range(2)]
    column = [[16 * chip + k for k in range(16)] for chip in range(32)]
    series = exchange(pack(samples).reshape(64, 64, 128), "tm")
    bins = dft(series.reshape(64, 4, 2, 8, 128))
    bands = exchange(bins.reshape(32, 128, 128), "tm", same_core)
    gathered = exchange(cross(bands), ("tm", "runs"), column)
    return moments(cohesion, rolling, gathered)


def solution(mesh):
    return jax.shard_map(
        per_device,
        mesh=mesh,
        in_specs=(P("runs", "tm", None), P(), P()),
        out_specs=(
            P(None, "tm", None, None, None),
            P(None, "tm", None, None),
            P(None, "tm", None, None, None),
        ),
        check_vma=False,
    )
```

```python
import functools
import math

import jax
import jax.numpy as jnp
import ml_dtypes
import numpy as np
from jax import lax
from jax.experimental import pallas as pl
from jax.experimental.pallas import tpu as pltpu
from jax.sharding import PartitionSpec as P

CH = 128
BIN = 1024
NC = 4
NQ = 4
TOTAL = 131072
RUNS = 16
NB = 64
T1 = 512
T2 = 256

NT = (((1,), (1,)), ((), ()))
MIB = 1 << 20
PITCH = 136
STEP = 136


def split_table(table):
    high = table.astype(ml_dtypes.bfloat16)
    low = (table - high.astype(np.float64)).astype(ml_dtypes.bfloat16)
    return high, low


@functools.lru_cache(maxsize=None)
def tables():
    even, odd = np.arange(0, 256, 2), np.arange(1, 256, 2)
    t1 = np.arange(256)

    def trig(k, t, period):
        angle = 2.0 * np.pi * (k[:, None] * t[None, :] % period) / period
        return np.cos(angle), np.sin(angle)

    cos_e, sin_e = trig(even, t1, T1)
    cos_o, sin_o = trig(odd, t1, T1)
    sin_e[0] = -np.cos(np.pi * (t1 % 2))
    first_even = np.concatenate([cos_e, -sin_e], axis=0)
    first_odd = np.concatenate([cos_o, -sin_o], axis=0)
    t2 = np.arange(T2)
    cos_t, sin_t = trig(np.concatenate([even, odd]), t2, TOTAL)
    near = np.arange(128)
    second = np.zeros((2, NB, 2, 2, 2, 128))
    edge = np.zeros((NB, 8, T2))
    for band in range(NB):
        for parity in range(2):
            for m, (k2, sign) in enumerate(
                [(2 * band + parity, 1.0), (254 + parity - 2 * band, -1.0)]
            ):
                a = 2.0 * np.pi * (k2 * near % T2) / T2
                second[parity, band, 0, m, 0] = np.cos(a)
                second[parity, band, 0, m, 1] = np.sin(a)
                second[parity, band, 1, m, 0] = -sign * np.sin(a)
                second[parity, band, 1, m, 1] = sign * np.cos(a)
        for half in range(2):
            for m in range(2):
                a = 2.0 * np.pi * ((2 * (2 * band + m) + half) * t2 % 512) / 512
                edge[band, 4 * half + m] = np.cos(a)
                edge[band, 4 * half + 2 + m] = -np.sin(a)
    t = np.arange(TOTAL).reshape(T1, T2)
    window = 0.5 - 0.5 * np.cos(2.0 * np.pi * t / TOTAL)

    def passes(table):
        high, low = split_table(table)
        return np.concatenate([high, high, low], axis=1)

    return (
        window.astype(np.float32),
        cos_t.astype(np.float32),
        sin_t.astype(np.float32),
        passes(first_even),
        passes(first_odd),
        passes(second[0].reshape(256, 256)),
        passes(second[1].reshape(256, 256)),
        passes(edge.reshape(NB * 8, T2)),
    )


def split(value):
    high = value.astype(jnp.bfloat16)
    low = (value - high.astype(jnp.float32)).astype(jnp.bfloat16)
    return high, low


def dot(a, b):
    return jnp.dot(a, b, preferred_element_type=jnp.float32)


def dot_nt(a, b):
    return lax.dot_general(a, b, NT, preferred_element_type=jnp.float32)


def pack_kernel(x_hbm, o_ref, landed, turned, sems):
    copies = [
        pltpu.make_async_copy(x_hbm.at[r, :, h], landed.at[r, h], sems.at[r, h])
        for r in range(2)
        for h in range(2)
    ]
    for copy in copies:
        copy.start()
    for r in range(2):
        for h in range(2):
            copies[2 * r + h].wait()
            for u in range(8):
                turned[r, h, u * STEP : u * STEP + 128, :] = landed[r, h, u].T
            for ch in range(CH):
                o_ref[ch % 32, r, ch // 32, h] = turned[r, h, pl.ds(ch, 8, stride=STEP), :]


def pack(samples):
    x = samples.reshape(2, 8, 2, 128, CH)
    return pl.pallas_call(
        pack_kernel,
        in_specs=[pl.BlockSpec(memory_space=pltpu.HBM)],
        out_specs=pl.BlockSpec(memory_space=pltpu.VMEM),
        out_shape=jax.ShapeDtypeStruct((32, 2, 4, 2, 8, 128), jnp.float32),
        scratch_shapes=[
            pltpu.VMEM((2, 2, 8, 128, CH), jnp.float32),
            pltpu.VMEM((2, 2, 9 * STEP, 128), jnp.float32),
            pltpu.SemaphoreType.DMA((2, 2)),
        ],
        compiler_params=pltpu.CompilerParams(vmem_limit_bytes=50 * MIB),
        name="pack",
    )(x)


def dft_kernel(
    x_ref, w_ref, c_ref, s_ref, fe_ref, fo_ref, se_ref, so_ref, edge_ref, o_ref, edge_in, middle
):
    edge_in[...] = jnp.zeros_like(edge_in)
    first_row = lax.broadcasted_iota(jnp.int32, (256, T2), 0) == 0
    upper = lax.broadcasted_iota(jnp.int32, (32, 8, 128), 1) < 4

    for i in range(4):
        halves = [x_ref[:, i, h].reshape(T1, 128) for h in range(2)]
        x = jnp.concatenate(halves, axis=1) * w_ref[...]
        xh, xl = split(x[:256] + x[256:])
        a_even = dot(fe_ref[:, :256], xl) + dot(
            fe_ref[:, 256:], jnp.concatenate([xh, xh], axis=0)
        )
        xh, xl = split(x[:256] - x[256:])
        a_odd = dot(fo_ref[:, :256], xl) + dot(
            fo_ref[:, 256:], jnp.concatenate([xh, xh], axis=0)
        )
        a_re = jnp.concatenate([a_even[:128], a_odd[:128]], axis=0)
        a_im = jnp.concatenate([a_even[128:], a_odd[128:]], axis=0)
        c, s = c_ref[...], s_ref[...]
        b_re = a_re * c + a_im * s
        b_im = a_im * c - a_re * s
        edge_in[i : i + 1, :] = b_re[:1]
        edge_in[i + 4 : i + 5, :] = b_im[:1]
        b_re = jnp.where(first_row, 0.0, b_re)
        b_im = jnp.where(first_row, 0.0, b_im)
        plus = jnp.concatenate(
            [b_re[:, :128] + b_re[:, 128:], b_im[:, :128] + b_im[:, 128:]], axis=1
        )
        minus = jnp.concatenate(
            [b_re[:, :128] - b_re[:, 128:], b_im[:, :128] - b_im[:, 128:]], axis=1
        )
        middle[i, 0, 0], middle[i, 0, 1] = split(plus)
        middle[i, 1, 0], middle[i, 1, 1] = split(minus)

    eh, el = split(edge_in[...])
    edge = dot_nt(edge_ref[:, :256], el) + dot_nt(
        edge_ref[:, 256:], jnp.concatenate([eh, eh], axis=1)
    )
    first_lane = lax.broadcasted_iota(jnp.int32, (512, 128), 1) == 0
    sub = lax.broadcasted_iota(jnp.int32, (512, 128), 0) % 8 < 4

    for i in range(4):
        bh, bl = middle[i, 0, 0], middle[i, 0, 1]
        o_even = dot_nt(se_ref[:, :256], bl) + dot_nt(
            se_ref[:, 256:], jnp.concatenate([bh, bh], axis=1)
        )
        bh, bl = middle[i, 1, 0], middle[i, 1, 1]
        o_odd = dot_nt(so_ref[:, :256], bl) + dot_nt(
            so_ref[:, 256:], jnp.concatenate([bh, bh], axis=1)
        )
        low = edge if i == 0 else pltpu.roll(edge, 128 - i, 1)
        extra = jnp.where(sub, low, pltpu.roll(edge, 124 - i, 1))
        extra = jnp.where(first_lane, extra, 0.0).reshape(32, 2, 8, 128)
        for half in range(2):
            lanes = slice(128 * half, 128 * half + 128)
            e = o_even[:, lanes].reshape(32, 8, 128)
            o = o_odd[:, lanes].reshape(32, 8, 128)
            first = jnp.where(upper, e, pltpu.roll(o, 4, 1))
            second = jnp.where(upper, pltpu.roll(e, 4, 1), o)
            o_ref[:, 0, i, half] = first + extra[:, 0] if half == 0 else first
            o_ref[:, 1, i, half] = second + extra[:, 1] if half == 0 else second


def dft(x):
    consts = [jnp.asarray(t) for t in tables()]
    vmem = pl.BlockSpec(memory_space=pltpu.VMEM)
    return pl.pallas_call(
        dft_kernel,
        in_specs=[vmem] * (1 + len(consts)),
        out_specs=vmem,
        out_shape=jax.ShapeDtypeStruct((NB // 2, 2, 4, 2, 8, 128), jnp.float32),
        scratch_shapes=[
            pltpu.VMEM((128, T2), jnp.float32),
            pltpu.VMEM((4, 2, 2, 256, 256), jnp.bfloat16),
        ],
        compiler_params=pltpu.CompilerParams(vmem_limit_bytes=24 * MIB),
        name="dft",
    )(x, *consts)


def cross_kernel(x_ref, o_ref, rows, *, scale):
    row = lax.broadcasted_iota(jnp.int32, (CH, CH), 0)
    col = lax.broadcasted_iota(jnp.int32, (CH, CH), 1)
    for chip in range(32):
        rows[chip * PITCH : chip * PITCH + 128, :] = x_ref[chip * 128 : chip * 128 + 128, :]
    for band in range(2):
        parts = []
        for part in range(2):
            for c in range(4):
                cols = [
                    rows[pl.ds((band * 4 + c) * 16 + half * 8 + part * 2 + m, 32, stride=PITCH), :]
                    for m in (0, 1, 4, 5)
                    for half in range(2)
                ]
                parts.append(jnp.concatenate(cols, axis=1))
        v = jnp.concatenate(parts, axis=0)
        vh, vl = split(v)
        mixed = dot_nt(vh, vl)
        g = dot_nt(vh, vh) + (mixed + mixed.T)
        real = g[:CH, :CH] + g[CH:, CH:]
        imag = g[CH:, :CH] - g[:CH, CH:]
        packed = jnp.where(row >= col, real, imag) * scale
        for y in range(8):
            o_ref[band * 8 + y] = packed


def cross(x):
    scale = 1.0 / (0.375 * BIN * TOTAL)
    return pl.pallas_call(
        functools.partial(cross_kernel, scale=scale),
        in_specs=[pl.BlockSpec(memory_space=pltpu.VMEM)],
        out_specs=pl.BlockSpec(memory_space=pltpu.VMEM),
        out_shape=jax.ShapeDtypeStruct((16, CH, CH), jnp.float32),
        scratch_shapes=[pltpu.VMEM((33 * PITCH, 128), jnp.float32)],
        compiler_params=pltpu.CompilerParams(vmem_limit_bytes=24 * MIB),
        name="cross",
    )(x.reshape(64 * 64, 128))


def moments_kernel(
    lev_vec, roll_vec, x_ref, lm_hbm, sp_hbm, rm_hbm, sums, rolls, squares, lm, sp, rm, sems
):
    row = lax.broadcasted_iota(jnp.int32, (CH, CH), 0)
    col = lax.broadcasted_iota(jnp.int32, (CH, CH), 1)
    levels, turns = lev_vec[...], roll_vec[...]
    order = [2 * (k % 8) + k // 8 for k in range(RUNS)]
    lev_ref = [levels[0, r] for r in order]
    roll_ref = [turns[0, r] for r in order]
    sums[...] = jnp.zeros_like(sums)
    rolls[...] = jnp.zeros_like(rolls)
    squares[...] = jnp.zeros_like(squares)

    def unpack(m):
        t = m.T
        real = jnp.where(row >= col, m, t)
        imag = jnp.where(row < col, m, jnp.where(row > col, -t, 0.0))
        return real, imag

    def count(values, level):
        total = jnp.sum((values == level).astype(jnp.float32), axis=1, keepdims=True)
        return jnp.maximum(total, 1.0)

    sends = []

    def send(source, target, kind, level):
        copy = pltpu.make_async_copy(source.at[level], target.at[level], sems.at[kind, level])
        copy.start()
        sends.append(copy)

    for r in range(RUNS):
        value = x_ref[r]
        rolls[roll_ref[r]] += value
        sums[lev_ref[r]] += value
    for q in range(NQ):
        rm[q, 0, 0], rm[q, 0, 1] = unpack(rolls[q] / count(turns, q))
        send(rm, rm_hbm, 0, q)
    for l in range(NC):
        mean = sums[l] / count(levels, l)
        sums[l] = mean
        lm[l, 0, 0], lm[l, 0, 1] = unpack(mean)
        send(lm, lm_hbm, 1, l)
    for r in range(RUNS):
        level = lev_ref[r]
        offset = x_ref[r] - sums[level]
        squares[level] += offset * offset
    for l in range(NC):
        s = squares[l]
        sp[l, 0] = BIN * jnp.where(row == col, s, s + s.T)
        send(sp, sp_hbm, 2, l)
    for copy in sends:
        copy.wait()


def moments(cohesion, rolling, x):
    vmem = pl.BlockSpec(memory_space=pltpu.VMEM)
    smem = pl.BlockSpec(memory_space=pltpu.SMEM)
    hbm = pl.BlockSpec(memory_space=pltpu.HBM)
    shapes = [(NC, 1, 2, CH, CH), (NC, 1, CH, CH), (NQ, 1, 2, CH, CH)]
    return pl.pallas_call(
        moments_kernel,
        in_specs=[vmem, vmem, vmem],
        out_specs=(hbm, hbm, hbm),
        out_shape=tuple(jax.ShapeDtypeStruct(shape, jnp.float32) for shape in shapes),
        scratch_shapes=[pltpu.VMEM((4, CH, CH), jnp.float32)] * 3
        + [pltpu.VMEM(shape, jnp.float32) for shape in shapes]
        + [pltpu.SemaphoreType.DMA((3, 4))],
        compiler_params=pltpu.CompilerParams(vmem_limit_bytes=16 * MIB),
        name="moments",
    )(cohesion.reshape(1, RUNS), rolling.reshape(1, RUNS), x)


def exchange(x, axis, groups=None):
    return lax.all_to_all(
        x, axis, split_axis=0, concat_axis=0, tiled=True, axis_index_groups=groups
    )


def per_device(samples, cohesion, rolling):
    same_core = [[2 * chip + core for chip in range(32)] for core in range(2)]
    column = [[16 * chip + k for k in range(16)] for chip in range(32)]
    series = exchange(pack(samples).reshape(64, 64, 128), "tm")
    bins = dft(series.reshape(64, 4, 2, 8, 128))
    bands = exchange(bins.reshape(32, 128, 128), "tm", same_core)
    gathered = exchange(cross(bands), ("tm", "runs"), column)
    return moments(cohesion, rolling, gathered)


def solution(mesh):
    return jax.shard_map(
        per_device,
        mesh=mesh,
        in_specs=(P("runs", "tm", None), P(), P()),
        out_specs=(
            P(None, "tm", None, None, None),
            P(None, "tm", None, None),
            P(None, "tm", None, None, None),
        ),
        check_vma=False,
    )
```
